512 devices in a mesh: dp: 4 (over z_hi), seq: 32 (over y, z_lo, core), tile: 4 (over x).
Axes of the slice: x: 4, y: 4, z: 16 (z_hi: 4, z_lo: 4; z = z_hi * 4 + z_lo), core: 2. Of those that a mesh axis runs over, the one named last changes fastest.
Arguments:
- latents: bfloat16 [4, 32, 512, 1152], P('dp', 'seq', 'tile'), may hold values from -6 to 6
- upstream: bfloat16 [4, 32, 512, 1152], P('dp', 'seq', 'tile'), may hold values from -6 to 6
- modulation: float32 [4, 2, 1152], P('dp'), may hold values from -0.5 to 6
- space_qkv: bfloat16 [1152, 1728], P(('dp', 'tile')), may hold values from -1 to 1
- space_out: bfloat16 [576, 1152], P(('dp', 'tile')), may hold values from -0.25 to 0.25
- time_qkv: bfloat16 [1152, 1728], P(('dp', 'tile')), may hold values from -1 to 1
- time_out: bfloat16 [576, 1152], P(('dp', 'tile')), may hold values from -0.25 to 0.25
- space_pattern: int32 [8, 4], P('tile'), may hold values 0 or 1
- time_mask: int32 [32, 32], replicated, may hold values 0 or 1
Outputs:
- result: bfloat16 [4, 32, 512, 1152], P('dp', 'seq', 'tile')
- start_grad: bfloat16 [4, 32, 512, 1152], P('dp', 'seq', 'tile')
- time_out_grad: float32 [576, 1152], P(('dp', 'tile'))
The draws below stay inside these ranges and needn't reach their ends.
All inputs are finite; a program needn't handle non-finite values. No bound on the sum of `space_pattern` on one device may be relied on, other than what follows from the above.
Results may differ from the reference program's by a relative error of at most 0.035.
Values may be sent and summed in bfloat16 or wider, within the bound.
A program may use at most 64 MiB of HBM per device.

```python
import jax
import jax.numpy as jnp
from jax import lax

D = 1152
HEADS = 8
HEAD_DIM = 72
SBLK = 64
CLIPS = 4
FRAMES = 32
PATCHES = 512


def qkv_columns(key):
    parts = jax.random.normal(key, (3, D, HEADS * HEAD_DIM), jnp.float32)
    parts = jnp.clip(parts, -6.0, 6.0)
    mixed = parts[1]
    whole = jnp.concatenate([parts[0], mixed, parts[2]], axis=1)
    return whole * D ** (-0.5)


def draw_modulation(key, part):
    key = jax.random.fold_in(key, 11)
    values = jax.random.uniform(key, (CLIPS, 2, D), jnp.float32, -0.5, 1.0)
    return values


def draw_space_qkv(key, part):
    key = jax.random.fold_in(key, 21)
    whole = qkv_columns(key)
    return whole.astype(jnp.bfloat16)


def draw_time_qkv(key, part):
    key = jax.random.fold_in(key, 31)
    whole = qkv_columns(key)
    return whole.astype(jnp.bfloat16)


def with_ends(values, own_key, smallest, largest):
    shape = values.shape
    spot = [jax.random.randint(jax.random.fold_in(own_key, axis), (), 0, shape[axis]) for axis in range(len(shape))]
    values = values.at[tuple(spot)].set(smallest)
    longest = shape.index(max(shape))
    spot[longest] = (spot[longest] + 1) % shape[longest]
    return values.at[tuple(spot)].set(largest)


def levels(own_key, shape, shards, smallest, largest):
    level, own = 1.0, jax.random.fold_in(own_key, 6)
    for axis_at, blocks in shards:
        steps = jnp.exp(jax.random.uniform(jax.random.fold_in(own, axis_at), (blocks,), jnp.float32, smallest / len(shards), largest / len(shards)))
        level = level * jnp.repeat(steps, shape[axis_at] // blocks).reshape([-1 if axis == axis_at else 1 for axis in range(len(shape))])
    return level


def scatter_about(own_key, dims, scale, most, cuts=(), kind=jnp.bfloat16):
    level = levels(own_key, dims, cuts, -0.22, 0.18) if cuts else 1.0
    entries = jax.random.normal(own_key, dims, jnp.float32) * scale * level
    return jnp.minimum(jnp.maximum(entries, -most), most).astype(kind)


def setup_inputs(seed: int = 0) -> dict:
    arg_keys = jax.random.split(jax.random.key(seed), 10)
    latents = scatter_about(arg_keys[0], (CLIPS, FRAMES, PATCHES, D), 1.0, 6.0, ((0, 4), (1, 32), (2, 4)))
    upstream = scatter_about(arg_keys[1], (CLIPS, FRAMES, PATCHES, D), 1.0, 6.0, ((0, 4), (1, 32), (2, 4)))
    modulation = draw_modulation(jax.random.fold_in(arg_keys[9], 71), 0)
    space_qkv = draw_space_qkv(jax.random.fold_in(arg_keys[9], 71), 0)
    space_out = scatter_about(arg_keys[4], (HEADS * HEAD_DIM, D), (HEADS * HEAD_DIM) ** -0.5, 0.25, ((0, 16),))
    time_qkv = draw_time_qkv(jax.random.fold_in(arg_keys[9], 71), 0)
    time_out = scatter_about(arg_keys[6], (HEADS * HEAD_DIM, D), (HEADS * HEAD_DIM) ** -0.5, 0.25, ((0, 16),))
    space_pattern = with_ends((jax.random.randint(arg_keys[7], (PATCHES // SBLK, 4), 0, 4) < 3).astype(jnp.int32), jax.random.fold_in(arg_keys[7], 1), 0, 1)
    time_mask = with_ends((jax.random.randint(arg_keys[8], (FRAMES, FRAMES), 0, 4) < 3).astype(jnp.int32), jax.random.fold_in(arg_keys[8], 1), 0, 1)
    return dict(latents=latents, upstream=upstream, modulation=modulation, space_qkv=space_qkv, space_out=space_out, time_qkv=time_qkv, time_out=time_out, space_pattern=space_pattern, time_mask=time_mask)


EPSILON = 1e-06
MASKED = -1e+30

def heads(rows):
    return rows.reshape(rows.shape[:-1] + (HEADS, HEAD_DIM))

def merged(rows):
    return rows.reshape(rows.shape[:-2] + (HEADS * HEAD_DIM,))

def split(rows):
    width = HEADS * HEAD_DIM
    return (heads(rows[..., :width]), heads(rows[..., width:2 * width]), heads(rows[..., 2 * width:]))

def project(rows, weight):
    flat = rows.reshape(-1, rows.shape[-1])
    out = jnp.dot(flat, weight, preferred_element_type=jnp.float32)
    return out.reshape(rows.shape[:-1] + (weight.shape[1],))

def norm_scale(values, gain):
    inverse = lax.rsqrt(lax.optimization_barrier(jnp.mean(values * values, axis=-1, keepdims=True)) + EPSILON)
    return (inverse, values * inverse * gain)

def norm_back(values, inverse, gain, grad):
    scaled = grad * gain
    cubed = inverse * inverse * inverse
    return inverse * scaled - values * cubed * lax.optimization_barrier(jnp.mean(scaled * values, axis=-1, keepdims=True))

def forms(lead):
    if lead:
        return ('cbqhe', 'cbkhe')
    return ('cqbhe', 'ckbhe')

def weights_of(query, keys, allowed, lead):
    qform, kform = forms(lead)
    scores = jnp.einsum(qform + ',' + kform + '->cbhqk', query.astype(jnp.float32), keys.astype(jnp.float32))
    scores = jnp.where(allowed, scores * HEAD_DIM ** (-0.5), MASKED)
    top = lax.optimization_barrier(jnp.max(scores, axis=-1, keepdims=True))
    raised = jnp.exp(scores - top)
    return raised / lax.optimization_barrier(jnp.sum(raised, axis=-1, keepdims=True))

def attend(query, keys, values, allowed, lead):
    qform, kform = forms(lead)
    probs = weights_of(query, keys, allowed, lead)
    rounded = probs.astype(jnp.bfloat16).astype(jnp.float32)
    out = jnp.einsum('cbhqk,' + kform + '->' + qform, rounded, values.astype(jnp.float32))
    return (out.astype(jnp.bfloat16), probs)

def attend_back(query, keys, values, probs, grad_out, lead):
    qform, kform = forms(lead)
    grad32 = grad_out.astype(jnp.float32)
    dprob = jnp.einsum(qform + ',' + kform + '->cbhqk', grad32, values.astype(jnp.float32))
    delta = lax.optimization_barrier(jnp.sum(probs * dprob, axis=-1, keepdims=True))
    dscore = (probs * (dprob - delta) * HEAD_DIM ** (-0.5)).astype(jnp.bfloat16).astype(jnp.float32)
    dquery = jnp.einsum('cbhqk,' + kform + '->' + qform, dscore, keys.astype(jnp.float32))
    dkeys = jnp.einsum('cbhqk,' + qform + '->' + kform, dscore, query.astype(jnp.float32))
    rounded = probs.astype(jnp.bfloat16).astype(jnp.float32)
    dvalues = jnp.einsum('cbhqk,' + qform + '->' + kform, rounded, grad32)
    return (dquery, dkeys, dvalues)

def space_ok(space_pattern):
    block = jnp.arange(PATCHES) // SBLK
    rel = block[None, :] - 2 * (block[:, None] // 2) + 1
    inside = (rel >= 0) & (rel < 4)
    picked = jnp.take_along_axis(space_pattern[block], jnp.clip(rel, 0, 3), axis=1)
    return inside & ((picked == 1) | (block[None, :] == block[:, None]))

def time_ok(time_mask):
    frame = jnp.arange(FRAMES)
    return (frame[None, :] == frame[:, None]) | (frame[None, :] < frame[:, None]) & (time_mask == 1)

def reference(latents, upstream, modulation, space_qkv, space_out, time_qkv, time_out, space_pattern, time_mask):
    width = HEADS * HEAD_DIM
    start = latents.astype(jnp.float32)
    gain_space = 1.0 + modulation[:, 0][:, None, None, :]
    gain_time = 1.0 + modulation[:, 1][:, None, None, :]
    inverse_space, normed = norm_scale(start, gain_space)
    space_rows = project(normed.astype(jnp.bfloat16), space_qkv).astype(jnp.bfloat16)
    space_mask = space_ok(space_pattern)[None, None, None]
    frames_flat = space_rows.reshape(CLIPS * FRAMES, PATCHES, 3 * width)

    def space_forward(block):
        query, keys, values = split(block[None, None])
        out, probs = attend(query, keys, values, space_mask, True)
        return merged(out)[0, 0]
    space_att = lax.map(space_forward, frames_flat).reshape(CLIPS, FRAMES, PATCHES, width)
    middle = start + project(space_att, space_out)
    inverse_time, normed_time = norm_scale(middle, gain_time)
    time_rows = project(normed_time.astype(jnp.bfloat16), time_qkv).astype(jnp.bfloat16)
    frame_mask = time_ok(time_mask)[None, None, None]
    time_query, time_keys, time_values = split(time_rows)
    time_heads, time_probs = attend(time_query, time_keys, time_values, frame_mask, False)
    time_att = merged(time_heads)
    result = (middle + project(time_att, time_out)).astype(jnp.bfloat16)
    flat_up = upstream.reshape(-1, D)
    time_out_grad = jnp.dot(time_att.reshape(-1, width).T, flat_up, preferred_element_type=jnp.float32)
    grad_att = project(upstream, time_out.T).astype(jnp.bfloat16)
    gq, gk, gv = attend_back(time_query, time_keys, time_values, time_probs, heads(grad_att), False)
    time_grads = jnp.concatenate([merged(gq), merged(gk), merged(gv)], axis=-1).astype(jnp.bfloat16)
    middle_grad = upstream.astype(jnp.float32) + norm_back(middle, inverse_time, gain_time, project(time_grads, time_qkv.T))
    space_grad_att = project(middle_grad.astype(jnp.bfloat16), space_out.T).astype(jnp.bfloat16)
    grads_flat = space_grad_att.reshape(CLIPS * FRAMES, PATCHES, width)

    def space_backward(pair):
        block, grad = pair
        query, keys, values = split(block[None, None])
        probs = weights_of(query, keys, space_mask, True)
        dq, dk, dv = attend_back(query, keys, values, probs, heads(grad[None, None]), True)
        return jnp.concatenate([merged(dq), merged(dk), merged(dv)], axis=-1)[0, 0].astype(jnp.bfloat16)
    space_grads = lax.map(space_backward, (frames_flat, grads_flat)).reshape(CLIPS, FRAMES, PATCHES, 3 * width)
    start_grad = middle_grad + norm_back(start, inverse_space, gain_space, project(space_grads, space_qkv.T))
    return (result, start_grad.astype(jnp.bfloat16), time_out_grad)
```

```python
import jax
import jax.numpy as jnp
from jax import lax
from jax.experimental import pallas as pl
from jax.experimental.pallas import tpu as pltpu
from jax.sharding import PartitionSpec as P

HEADS = 8
HEAD_DIM = 72


EPSILON = 1e-06
MASKED = -1e30


def extended(block, sides, width):
    for axis, dim in sides:
        count = lax.axis_size(axis)
        forward = [(i, i + 1) for i in range(count - 1)]
        backward = [(target, source) for source, target in forward]
        low = lax.ppermute(
            lax.slice_in_dim(block, block.shape[dim] - width, None, axis=dim), axis, forward
        )
        high = lax.ppermute(lax.slice_in_dim(block, 0, width, axis=dim), axis, backward)
        block = jnp.concatenate([low, block, high], axis=dim)
    return block


def shifted(array, axis, by):
    devices = lax.axis_size(axis)
    pairs = [(i, i + by) for i in range(devices) if 0 <= i + by < devices]
    return lax.ppermute(array, axis, pairs)


def heads(rows):
    return rows.reshape(rows.shape[:-1] + (HEADS, HEAD_DIM))


def merged(rows):
    return rows.reshape(rows.shape[:-2] + (HEADS * HEAD_DIM,))


def split(rows):
    width = HEADS * HEAD_DIM
    return (
        heads(rows[..., :width]),
        heads(rows[..., width : 2 * width]),
        heads(rows[..., 2 * width :]),
    )


def project(rows, weight):
    flat = rows.reshape(-1, rows.shape[-1])
    out = jnp.dot(flat, weight, preferred_element_type=jnp.float32)
    return out.reshape(rows.shape[:-1] + (weight.shape[1],))


def project_back(rows, weight):
    flat = rows.reshape(-1, rows.shape[-1])
    out = jnp.einsum("rk,dk->rd", flat, weight, preferred_element_type=jnp.float32)
    return out.reshape(rows.shape[:-1] + (weight.shape[0],))


def norm_scale(values, gain):
    inverse = lax.rsqrt(jnp.mean(values * values, axis=-1, keepdims=True) + EPSILON)
    return (inverse, values * inverse * gain)


def norm_back(values, inverse, gain, grad):
    scaled = grad * gain
    cubed = inverse * inverse * inverse
    return inverse * scaled - values * cubed * jnp.mean(scaled * values, axis=-1, keepdims=True)


def forms(lead):
    if lead:
        return ("cbqhe", "cbkhe")
    return ("cqbhe", "ckbhe")


def weights_of(query, keys, allowed, lead):
    qform, kform = forms(lead)
    scores = jnp.einsum(
        qform + "," + kform + "->cbhqk", query, keys, preferred_element_type=jnp.float32
    )
    scores = jnp.where(allowed, scores * HEAD_DIM ** (-0.5), MASKED)
    top = jnp.max(scores, axis=-1, keepdims=True)
    raised = jnp.exp(scores - top)
    return raised / jnp.sum(raised, axis=-1, keepdims=True)


def attend(query, keys, values, allowed, lead):
    qform, kform = forms(lead)
    probs = weights_of(query, keys, allowed, lead)
    out = jnp.einsum(
        "cbhqk," + kform + "->" + qform,
        probs.astype(jnp.bfloat16),
        values,
        preferred_element_type=jnp.float32,
    )
    return (out.astype(jnp.bfloat16), probs)


def attend_back(query, keys, values, probs, grad_out, lead):
    qform, kform = forms(lead)
    dprob = jnp.einsum(
        qform + "," + kform + "->cbhqk", grad_out, values, preferred_element_type=jnp.float32
    )
    delta = jnp.sum(probs * dprob, axis=-1, keepdims=True)
    dscore = (probs * (dprob - delta) * HEAD_DIM ** (-0.5)).astype(jnp.bfloat16)
    dquery = jnp.einsum(
        "cbhqk," + kform + "->" + qform, dscore, keys, preferred_element_type=jnp.float32
    )
    dkeys = jnp.einsum(
        "cbhqk," + qform + "->" + kform, dscore, query, preferred_element_type=jnp.float32
    )
    dvalues = jnp.einsum(
        "cbhqk," + qform + "->" + kform,
        probs.astype(jnp.bfloat16),
        grad_out,
        preferred_element_type=jnp.float32,
    )
    return (dquery, dkeys, dvalues)


def time_ok(time_mask):
    frame = jnp.arange(time_mask.shape[0])
    return (frame[None, :] == frame[:, None]) | (frame[None, :] < frame[:, None]) & (time_mask == 1)


MESH = pl.DeviceIdType.MESH
LANES = (896, 640, 896)


def coords():
    dp, seq, tile = lax.axis_index("dp"), lax.axis_index("seq"), lax.axis_index("tile")
    return dp, seq // 8, (seq // 2) % 4, seq % 2, tile


def at(dp, y, zl, core, tile):
    return (dp, (y * 4 + zl) * 2 + core, tile)


class Gather:
    def __init__(self, bufs, send, recv):
        self.bufs, self.send, self.recv = bufs, send, recv
        dp, y, zl, core, x = self.pos = coords()
        self.first = core == 0
        self.p1 = jnp.where(self.first, y, x)
        self.p2 = jnp.where(self.first, x, y)
        self.q2 = jnp.where(self.first, y, x)

    def own(self, g):
        return self.bufs[g].at[self.pos[3], self.p2, self.p1]

    def along1(self, place):
        dp, y, zl, core, x = self.pos
        place = lax.rem(place + 4, 4)
        return at(dp, jnp.where(self.first, place, y), zl, core, jnp.where(self.first, x, place))

    def along2(self, place):
        dp, y, zl, core, x = self.pos
        place = lax.rem(place + 4, 4)
        return at(dp, jnp.where(self.first, y, place), zl, core, jnp.where(self.first, place, x))

    def copy(self, g, ref, slot, target, recv_slot=None):
        return pltpu.make_async_remote_copy(
            src_ref=ref,
            dst_ref=ref,
            send_sem=self.send.at[g, slot],
            recv_sem=self.recv.at[g, slot if recv_slot is None else recv_slot],
            device_id=target,
            device_id_type=MESH,
        )

    def third(self, g, zl):
        return self.own(g).at[pl.ds(3 * zl, 3)]

    def zsend(self, g):
        dp, y, zl, core, x = self.pos

        @pl.when((dp == y) & (zl < 3))
        def _():
            for k in range(1, 4):
                self.copy(g, self.third(g, zl), k - 1, at(lax.rem(dp + k, 4), y, zl, core, x), 0).start()

    def zpass(self, g):
        dp, y, zl, core, x = self.pos

        @pl.when((dp != y) & (zl < 3))
        def _():
            self.copy(g, self.third(g, zl), 0, self.pos_id(), 0).wait_recv()
            for k in range(1, 4):
                target = at(dp, y, lax.rem(zl + k, 4), core, x)
                self.copy(g, self.third(g, zl), k - 1, target, 1 + zl).start()

    def pos_id(self):
        dp, y, zl, core, x = self.pos
        return at(dp, y, zl, core, x)

    def zdone(self, g):
        dp, y, zl, core, x = self.pos
        for source in range(3):

            @pl.when((dp != y) & (zl != source))
            def _():
                self.copy(g, self.third(g, source), 0, self.pos_id(), 1 + source).wait_recv()

    def zend(self, g):
        dp, y, zl, core, x = self.pos

        @pl.when(zl < 3)
        def _():
            for k in range(3):
                self.copy(g, self.third(g, zl), k, self.pos_id()).wait_send()

    def one(self, g, place):
        return self.bufs[g].at[self.pos[3], self.p2, lax.rem(place + 4, 4)]

    def bundle(self, g, place):
        return self.bufs[g].at[self.pos[3], lax.rem(place + 4, 4)]

    def ring_send(self, g, part, along, p, slot):
        self.copy(g, part(g, p), slot, along(p + 1)).start()
        self.copy(g, part(g, p), slot + 1, along(p - 1)).start()

    def ring_pass(self, g, part, along, p, slot, cut, size):
        low, high = pl.ds(0, cut), pl.ds(cut, size - cut)
        self.copy(g, part(g, p - 1), slot, along(p)).wait_recv()
        self.copy(g, part(g, p - 1).at[low], slot + 2, along(p + 1)).start()
        self.copy(g, part(g, p + 1), slot + 1, along(p)).wait_recv()
        self.copy(g, part(g, p + 1).at[high], slot + 3, along(p - 1)).start()

    def ring_done(self, g, part, along, p, slot, cut, size):
        low, high = pl.ds(0, cut), pl.ds(cut, size - cut)
        self.copy(g, part(g, p + 2).at[low], slot + 2, along(p)).wait_recv()
        self.copy(g, part(g, p + 2).at[high], slot + 3, along(p)).wait_recv()

    def ring_end(self, g, part, along, p, slot, cut, size):
        low, high = pl.ds(0, cut), pl.ds(cut, size - cut)
        self.copy(g, part(g, p), slot, along(p)).wait_send()
        self.copy(g, part(g, p), slot + 1, along(p)).wait_send()
        self.copy(g, part(g, p - 1).at[low], slot + 2, along(p)).wait_send()
        self.copy(g, part(g, p + 1).at[high], slot + 3, along(p)).wait_send()

    def s1send(self, g):
        self.zdone(g)
        self.ring_send(g, self.one, self.along1, self.p1, 4)

    def s1pass(self, g):
        self.ring_pass(g, self.one, self.along1, self.p1, 4, 5, 9)

    def s2send(self, g):
        self.ring_done(g, self.one, self.along1, self.p1, 4, 5, 9)
        self.ring_send(g, self.bundle, self.along2, self.p2, 8)
        self.twin(g, 0)

    def s2pass(self, g):
        self.ring_pass(g, self.bundle, self.along2, self.p2, 8, 2, 4)
        self.twin(g, -1)
        self.twin(g, 1)

    def s2done(self, g):
        self.ring_done(g, self.bundle, self.along2, self.p2, 8, 2, 4)
        self.twin(g, 2)

    def twin(self, g, step):
        dp, y, zl, core, x = self.pos
        self.copy(g, self.bundle(g, self.p2 + step), 13 + step, at(dp, y, zl, 1 - core, x)).start()

    def end(self, g):
        dp, y, zl, core, x = self.pos
        for step in (0, -1, 1, 2):
            ref = self.bufs[g].at[1 - core, lax.rem(self.q2 + step + 4, 4)]
            self.copy(g, ref, 13 + step, self.pos_id()).wait_recv()

    def drain(self, g):
        self.zend(g)
        self.ring_end(g, self.one, self.along1, self.p1, 4, 5, 9)
        self.ring_end(g, self.bundle, self.along2, self.p2, 8, 2, 4)
        for step in (0, -1, 1, 2):
            self.copy(g, self.bundle(g, self.p2 + step), 13 + step, self.pos_id()).wait_send()


def greet():
    dp, y, zl, core, x = coords()
    barrier = pltpu.get_barrier_semaphore()
    others = [at(lax.rem(dp + k, 4), y, zl, core, x) for k in range(1, 4)]
    others += [at(dp, lax.rem(y + k, 4), zl, core, x) for k in range(1, 4)]
    others += [at(dp, y, lax.rem(zl + k, 4), core, x) for k in range(1, 4)]
    others += [at(dp, y, zl, core, lax.rem(x + k, 4)) for k in range(1, 4)]
    others += [at(dp, y, zl, 1 - core, x)]
    for target in others:
        pl.semaphore_signal(barrier, inc=1, device_id=target, device_id_type=MESH)
    pl.semaphore_wait(barrier, len(others))


def place_own(gather, space_qkv, space_out, time_qkv, time_out):
    dp, y, zl, core, x = gather.pos
    for half in range(2):

        @pl.when((dp == y) & (core == half))
        def _():
            for g, ref in ((0, space_qkv), (2, time_qkv)):
                if half == 0:
                    block = ref[:, :896]
                else:
                    block = jnp.concatenate([ref[:, 896:], jnp.zeros((72, 64), jnp.bfloat16)], axis=1)
                gather.own(g)[...] = block.reshape(9, 8, 896)
            block = jnp.concatenate(
                [space_out[...].astype(jnp.float32), time_out[...].astype(jnp.float32)], axis=0
            )
            if half == 0:
                block = block[:, :640]
            else:
                block = jnp.concatenate([block[:, 640:], jnp.zeros((72, 128), jnp.float32)], axis=1)
            gather.own(1)[...] = block.astype(jnp.bfloat16).reshape(9, 8, 640)


def gather_kernel(space_qkv, space_out, time_qkv, time_out, w0, w1, w2, send, recv):
    gather = Gather((w0, w1, w2), send, recv)
    place_own(gather, space_qkv, space_out, time_qkv, time_out)
    greet()
    for g in range(3):
        gather.zsend(g)
    gather.zpass(0)
    gather.s1send(0)
    gather.zpass(1)
    gather.s1pass(0)
    gather.s2send(0)
    gather.s1send(1)
    gather.zpass(2)
    gather.s1pass(1)
    gather.s2pass(0)
    gather.s2send(1)
    gather.s1send(2)
    gather.s2done(0)
    gather.s1pass(2)
    gather.s2pass(1)
    gather.s2send(2)
    gather.s2done(1)
    gather.s2pass(2)
    gather.s2done(2)
    for g in range(3):
        gather.end(g)
    for g in range(3):
        gather.drain(g)


def gathered(space_qkv, space_out, time_qkv, time_out):
    w0, w1, w2 = pl.pallas_call(
        gather_kernel,
        out_shape=[jax.ShapeDtypeStruct((2, 4, 4, 9, 8, lanes), jnp.bfloat16) for lanes in LANES],
        in_specs=[pl.BlockSpec(memory_space=pltpu.VMEM)] * 4,
        out_specs=[pl.BlockSpec(memory_space=pltpu.VMEM)] * 3,
        scratch_shapes=[pltpu.SemaphoreType.DMA((3, 16)), pltpu.SemaphoreType.DMA((3, 16))],
        compiler_params=pltpu.CompilerParams(
            collective_id=0, has_side_effects=True, vmem_limit_bytes=60 << 20
        ),
    )(space_qkv, space_out, time_qkv, time_out)

    def whole(buf):
        lanes = buf.shape[-1]
        first = buf[0].transpose(1, 0, 2, 3, 4).reshape(1152, lanes)
        return jnp.concatenate([first, buf[1].reshape(1152, lanes)], axis=1)

    outs = whole(w1)[:, :1152].reshape(16, 72, 1152)
    return (
        whole(w0)[:, :1728],
        outs[:, :36].reshape(576, 1152),
        whole(w2)[:, :1728],
        outs[:, 36:].reshape(576, 1152),
    )


def local(
    latents,
    upstream,
    modulation,
    space_qkv,
    space_out,
    time_qkv,
    time_out,
    space_pattern,
    time_mask,
):
    width = HEADS * HEAD_DIM
    own = latents.shape[2]
    span = own // 2
    space_qkv_all, space_out_all, time_qkv_all, time_out_all = gathered(
        space_qkv, space_out, time_qkv, time_out
    )
    start = latents.astype(jnp.float32)
    gain_space = 1.0 + modulation[:, 0][:, None, None, :]
    gain_time = 1.0 + modulation[:, 1][:, None, None, :]
    inverse_space, normed = norm_scale(start, gain_space)
    space_rows = project(normed.astype(jnp.bfloat16), space_qkv_all).astype(jnp.bfloat16)
    query = heads(space_rows[..., :width])
    window = extended(space_rows[..., width:], (("tile", 2),), span)
    keys = heads(window[..., :width])
    values = heads(window[..., width:])
    tile_at = lax.axis_index("tile")
    tiles = lax.axis_size("tile")
    slots = jnp.arange(4)
    block_ok = (space_pattern == 1) | (slots[None, :] == jnp.arange(2)[:, None] + 1)
    global_block = 2 * tile_at - 1 + slots
    block_ok = block_ok & ((global_block >= 0) & (global_block < 2 * tiles))[None, :]
    allowed = jnp.repeat(jnp.repeat(block_ok, span, axis=0), span, axis=1)[None, None, None]
    space_heads, space_probs = attend(query, keys, values, allowed, True)
    space_att = merged(space_heads)
    middle = start + project(space_att, space_out_all)
    inverse_time, normed_time = norm_scale(middle, gain_time)
    normed_time = normed_time.astype(jnp.bfloat16)
    frame_mask = time_ok(time_mask)[None, None, None]
    time_local = project(normed_time, time_qkv_all).astype(jnp.bfloat16)
    rows = lax.all_to_all(time_local, "seq", split_axis=2, concat_axis=1, tiled=True)
    time_query, time_keys, time_values = split(rows)
    out, probs = attend(time_query, time_keys, time_values, frame_mask, False)
    time_patches = merged(out)
    time_att = lax.all_to_all(time_patches, "seq", split_axis=1, concat_axis=2, tiled=True)
    result = (middle + project(time_att, time_out_all)).astype(jnp.bfloat16)
    flat_up = upstream.reshape(-1, upstream.shape[-1])
    term = jnp.einsum(
        "rh,rd->hd", time_att.reshape(-1, width), flat_up, preferred_element_type=jnp.float32
    )
    rows_part = lax.psum_scatter(
        term.astype(jnp.bfloat16), ("dp", "tile"), scatter_dimension=0, tiled=True
    )
    time_out_grad = lax.psum(rows_part, "seq").astype(jnp.float32)
    grad_att = project_back(upstream, time_out_all).astype(jnp.bfloat16)
    grad_patches = lax.all_to_all(grad_att, "seq", split_axis=2, concat_axis=1, tiled=True)
    time_query, time_keys, time_values = split(rows)
    time_probs = weights_of(time_query, time_keys, frame_mask, False)
    gq, gk, gv = attend_back(
        time_query, time_keys, time_values, time_probs, heads(grad_patches), False
    )
    patch_grads = jnp.concatenate([merged(gq), merged(gk), merged(gv)], axis=-1).astype(
        jnp.bfloat16
    )
    time_grads = lax.all_to_all(patch_grads, "seq", split_axis=1, concat_axis=2, tiled=True)
    middle_grad = upstream.astype(jnp.float32) + norm_back(
        middle, inverse_time, gain_time, project_back(time_grads, time_qkv_all)
    )
    space_grad_att = project_back(middle_grad.astype(jnp.bfloat16), space_out_all).astype(
        jnp.bfloat16
    )
    dq, dk, dv = attend_back(query, keys, values, space_probs, heads(space_grad_att), True)
    rim = jnp.concatenate([merged(dk), merged(dv)], axis=-1)
    from_right = shifted(rim[:, :, :span].astype(jnp.bfloat16), "tile", -1).astype(jnp.float32)
    from_left = shifted(rim[:, :, span + own :].astype(jnp.bfloat16), "tile", 1).astype(jnp.float32)
    own_grads = rim[:, :, span : span + own] + jnp.concatenate([from_left, from_right], axis=2)
    space_grads = jnp.concatenate([merged(dq), own_grads], axis=-1).astype(jnp.bfloat16)
    start_grad = middle_grad + norm_back(
        start, inverse_space, gain_space, project_back(space_grads, space_qkv_all)
    )
    return (result, start_grad.astype(jnp.bfloat16), time_out_grad)


def solution(mesh):
    in_specs = (
        P("dp", "seq", "tile", None),
        P("dp", "seq", "tile", None),
        P("dp", None, None),
        P(("dp", "tile"), None),
        P(("dp", "tile"), None),
        P(("dp", "tile"), None),
        P(("dp", "tile"), None),
        P("tile", None),
        P(),
    )
    out_specs = (
        P("dp", "seq", "tile", None),
        P("dp", "seq", "tile", None),
        P(("dp", "tile"), None),
    )
    return jax.shard_map(local, mesh=mesh, in_specs=in_specs, out_specs=out_specs, check_vma=False)
```

```python
import jax
import jax.numpy as jnp
from jax import lax
from jax.experimental import pallas as pl
from jax.experimental.pallas import tpu as pltpu
from jax.sharding import PartitionSpec as P

HEADS = 8
HEAD_DIM = 72
WIDTH = HEADS * HEAD_DIM
WIDE = 640
D = 1152
ROWS = 128
EPSILON = 1e-06
MASKED = -1e30
SCALE = HEAD_DIM ** (-0.5)
BF16 = jnp.bfloat16
F32 = jnp.float32

MESH = pl.DeviceIdType.MESH
LANES = (896, 640, 896)


def coords():
    dp, seq, tile = lax.axis_index("dp"), lax.axis_index("seq"), lax.axis_index("tile")
    return dp, seq // 8, (seq // 2) % 4, seq % 2, tile


def at(dp, y, zl, core, tile):
    return (dp, (y * 4 + zl) * 2 + core, tile)


class Gather:
    def __init__(self, bufs, send, recv):
        self.bufs, self.send, self.recv = bufs, send, recv
        dp, y, zl, core, x = self.pos = coords()
        self.first = core == 0
        self.p1 = jnp.where(self.first, y, x)
        self.p2 = jnp.where(self.first, x, y)
        self.q2 = jnp.where(self.first, y, x)

    def own(self, g):
        return self.bufs[g].at[self.pos[3], self.p2, self.p1]

    def along1(self, place):
        dp, y, zl, core, x = self.pos
        place = lax.rem(place + 4, 4)
        return at(dp, jnp.where(self.first, place, y), zl, core, jnp.where(self.first, x, place))

    def along2(self, place):
        dp, y, zl, core, x = self.pos
        place = lax.rem(place + 4, 4)
        return at(dp, jnp.where(self.first, y, place), zl, core, jnp.where(self.first, place, x))

    def copy(self, g, ref, slot, target, recv_slot=None):
        return pltpu.make_async_remote_copy(
            src_ref=ref,
            dst_ref=ref,
            send_sem=self.send.at[g, slot],
            recv_sem=self.recv.at[g, slot if recv_slot is None else recv_slot],
            device_id=target,
            device_id_type=MESH,
        )

    def third(self, g, zl):
        return self.own(g).at[pl.ds(3 * zl, 3)]

    def zsend(self, g):
        dp, y, zl, core, x = self.pos

        @pl.when((dp == y) & (zl < 3))
        def _():
            for k in range(1, 4):
                self.copy(g, self.third(g, zl), k - 1, at(lax.rem(dp + k, 4), y, zl, core, x), 0).start()

    def zpass(self, g):
        dp, y, zl, core, x = self.pos

        @pl.when((dp != y) & (zl < 3))
        def _():
            self.copy(g, self.third(g, zl), 0, self.pos_id(), 0).wait_recv()
            for k in range(1, 4):
                target = at(dp, y, lax.rem(zl + k, 4), core, x)
                self.copy(g, self.third(g, zl), k - 1, target, 1 + zl).start()

    def pos_id(self):
        dp, y, zl, core, x = self.pos
        return at(dp, y, zl, core, x)

    def zdone(self, g):
        dp, y, zl, core, x = self.pos
        for source in range(3):

            @pl.when((dp != y) & (zl != source))
            def _():
                self.copy(g, self.third(g, source), 0, self.pos_id(), 1 + source).wait_recv()

    def zend(self, g):
        dp, y, zl, core, x = self.pos

        @pl.when(zl < 3)
        def _():
            for k in range(3):
                self.copy(g, self.third(g, zl), k, self.pos_id()).wait_send()

    def one(self, g, place):
        return self.bufs[g].at[self.pos[3], self.p2, lax.rem(place + 4, 4)]

    def bundle(self, g, place):
        return self.bufs[g].at[self.pos[3], lax.rem(place + 4, 4)]

    def ring_send(self, g, part, along, p, slot):
        self.copy(g, part(g, p), slot, along(p + 1)).start()
        self.copy(g, part(g, p), slot + 1, along(p - 1)).start()

    def ring_pass(self, g, part, along, p, slot, cut, size):
        low, high = pl.ds(0, cut), pl.ds(cut, size - cut)
        self.copy(g, part(g, p - 1), slot, along(p)).wait_recv()
        self.copy(g, part(g, p - 1).at[low], slot + 2, along(p + 1)).start()
        self.copy(g, part(g, p + 1), slot + 1, along(p)).wait_recv()
        self.copy(g, part(g, p + 1).at[high], slot + 3, along(p - 1)).start()

    def ring_done(self, g, part, along, p, slot, cut, size):
        low, high = pl.ds(0, cut), pl.ds(cut, size - cut)
        self.copy(g, part(g, p + 2).at[low], slot + 2, along(p)).wait_recv()
        self.copy(g, part(g, p + 2).at[high], slot + 3, along(p)).wait_recv()

    def ring_end(self, g, part, along, p, slot, cut, size):
        low, high = pl.ds(0, cut), pl.ds(cut, size - cut)
        self.copy(g, part(g, p), slot, along(p)).wait_send()
        self.copy(g, part(g, p), slot + 1, along(p)).wait_send()
        self.copy(g, part(g, p - 1).at[low], slot + 2, along(p)).wait_send()
        self.copy(g, part(g, p + 1).at[high], slot + 3, along(p)).wait_send()

    def s1send(self, g):
        self.zdone(g)
        self.ring_send(g, self.one, self.along1, self.p1, 4)

    def s1pass(self, g):
        self.ring_pass(g, self.one, self.along1, self.p1, 4, 5, 9)

    def s2send(self, g):
        self.ring_done(g, self.one, self.along1, self.p1, 4, 5, 9)
        self.ring_send(g, self.bundle, self.along2, self.p2, 8)
        self.twin(g, 0)

    def s2pass(self, g):
        self.ring_pass(g, self.bundle, self.along2, self.p2, 8, 2, 4)
        self.twin(g, -1)
        self.twin(g, 1)

    def s2done(self, g):
        self.ring_done(g, self.bundle, self.along2, self.p2, 8, 2, 4)
        self.twin(g, 2)

    def twin(self, g, step):
        dp, y, zl, core, x = self.pos
        self.copy(g, self.bundle(g, self.p2 + step), 13 + step, at(dp, y, zl, 1 - core, x)).start()

    def end(self, g):
        dp, y, zl, core, x = self.pos
        for step in (0, -1, 1, 2):
            ref = self.bufs[g].at[1 - core, lax.rem(self.q2 + step + 4, 4)]
            self.copy(g, ref, 13 + step, self.pos_id()).wait_recv()

    def drain(self, g):
        self.zend(g)
        self.ring_end(g, self.one, self.along1, self.p1, 4, 5, 9)
        self.ring_end(g, self.bundle, self.along2, self.p2, 8, 2, 4)
        for step in (0, -1, 1, 2):
            self.copy(g, self.bundle(g, self.p2 + step), 13 + step, self.pos_id()).wait_send()


def greet():
    dp, y, zl, core, x = coords()
    barrier = pltpu.get_barrier_semaphore()
    others = [at(lax.rem(dp + k, 4), y, zl, core, x) for k in range(1, 4)]
    others += [at(dp, lax.rem(y + k, 4), zl, core, x) for k in range(1, 4)]
    others += [(dp, y * 8 + lax.rem(zl * 2 + core + k, 8), x) for k in range(1, 8)]
    others += [at(dp, y, zl, core, lax.rem(x + k, 4)) for k in range(1, 4)]
    for target in others:
        pl.semaphore_signal(barrier, inc=1, device_id=target, device_id_type=MESH)
    pl.semaphore_wait(barrier, len(others))


def place_own(gather, space_qkv, space_out, time_qkv, time_out):
    dp, y, zl, core, x = gather.pos
    for half in range(2):

        @pl.when((dp == y) & (core == half))
        def _():
            for g, ref in ((0, space_qkv), (2, time_qkv)):
                if half == 0:
                    block = ref[:, :896]
                else:
                    block = jnp.concatenate([ref[:, 896:], jnp.zeros((72, 64), jnp.bfloat16)], axis=1)
                gather.own(g)[...] = block.reshape(9, 8, 896)
            block = jnp.concatenate(
                [space_out[...].astype(jnp.float32), time_out[...].astype(jnp.float32)], axis=0
            )
            if half == 0:
                block = block[:, :640]
            else:
                block = jnp.concatenate([block[:, 640:], jnp.zeros((72, 128), jnp.float32)], axis=1)
            gather.own(1)[...] = block.astype(jnp.bfloat16).reshape(9, 8, 640)

def rem4(value):
    return lax.rem(value + 4, 4)


class Exchange:
    def __init__(self, n, me, target, block, slot, send, recv):
        self.n, self.me, self.target = n, me, target
        self.block, self.slot, self.sems = block, slot, (send, recv)

    def copy(self, k, src, dst, target):
        return pltpu.make_async_remote_copy(
            src_ref=src,
            dst_ref=dst,
            send_sem=self.sems[0].at[k - 1],
            recv_sem=self.sems[1].at[k - 1],
            device_id=target,
            device_id_type=MESH,
        )

    def start(self):
        for k in range(1, self.n):
            other = lax.rem(self.me + k, self.n)
            self.copy(k, self.block(other), self.slot(self.me), self.target(other)).start()

    def wait(self):
        for k in range(1, self.n):
            source = lax.rem(self.me + self.n - k, self.n)
            self.copy(k, self.slot(source), self.slot(source), self.target(source)).wait_recv()

    def drain(self):
        for k in range(1, self.n):
            other = lax.rem(self.me + k, self.n)
            self.copy(k, self.block(other), self.slot(self.me), self.target(other)).wait_send()


def rows_at(ref, size, index):
    return ref.at[pl.ds(pl.multiple_of(index * size, size), size)]


def dot(a, b):
    return jnp.dot(a, b, preferred_element_type=F32)


def dot_nt(a, b):
    return lax.dot_general(a, b, (((1,), (1,)), ((), ())), preferred_element_type=F32)


def dot_tn(a, b):
    return lax.dot_general(a, b, (((0,), (0,)), ((), ())), preferred_element_type=F32)


def iota(shape, axis):
    return lax.broadcasted_iota(jnp.int32, shape, axis)


def shuffle():
    new, old = iota((ROWS, ROWS), 0), iota((ROWS, ROWS), 1)
    source = ((new >> 2) & 7) * 16 + (new >> 5) * 4 + (new & 3)
    return (source == old).astype(F32).astype(BF16)


class Move:
    def __init__(self, out, source, first, middle, last, sems, slot):
        dp, y, zl, core, x = coords()
        t = zl * 2 + core
        self.out, self.source, self.first, self.middle, self.last = out, source, first, middle, last
        self.y, self.t = y, t
        near = lambda n, other: (dp, y * 8 + other, x)
        far = lambda n, other: (dp, other * 8 + t, x)
        send, recv = sems
        legs = ((8, t, near, 16), (4, y, far, 32))
        if not out:
            legs = legs[::-1]
        self.sizes = (legs[0][3], legs[1][3])
        self.mine = (legs[0][1], legs[1][1])
        self.legs = []
        for leg, (src, dst) in enumerate(((source, first), (middle, last))):
            n, me, target, size = legs[leg]
            self.legs.append(
                Exchange(
                    n,
                    me,
                    lambda other, target=target, n=n: target(n, other),
                    lambda other, src=src, size=size: rows_at(src, size, other),
                    lambda index, dst=dst, size=size: rows_at(dst, size, index),
                    send.at[slot, leg],
                    recv.at[slot, leg],
                )
            )

    def keep(self, leg, src, dst):
        size, me = self.sizes[leg], self.mine[leg]
        rows_at(dst, size, me)[...] = rows_at(src, size, me)[...]

    def start(self):
        self.legs[0].start()
        self.keep(0, self.source, self.first)

    def turn(self, order):
        self.legs[0].wait()
        if self.out:
            mixed = dot(order, self.first[...])
        else:
            mixed = dot_tn(order, self.first[...])
        self.middle[...] = mixed.astype(BF16)
        self.legs[1].start()
        self.keep(1, self.middle, self.last)

    def finish(self):
        self.legs[1].wait()

    def drain(self):
        self.legs[0].drain()
        self.legs[1].drain()


def inverse_of(values):
    return lax.rsqrt(jnp.sum(values * values, axis=-1, keepdims=True) * (1.0 / D) + EPSILON)


def norm_back(values, inverse, gain, grad):
    scaled = grad * gain
    cubed = inverse * inverse * inverse
    mean = jnp.sum(scaled * values, axis=-1, keepdims=True) * (1.0 / D)
    return inverse * scaled - values * (cubed * mean)


def span(h):
    low, high = h * HEAD_DIM, (h + 1) * HEAD_DIM
    begin, end = low // 128 * 128, -(-high // 128) * 128
    lane = iota((1, end - begin), 1) + begin
    keep = ((lane >= low) & (lane < high)).astype(F32).astype(BF16)
    return slice(begin, end), keep


def attend(q, k, v, bias, probs, out):
    out[...] = jnp.zeros_like(out)
    for h in range(HEADS):
        lanes, keep = span(h)
        scores = dot_nt(q[:, lanes] * keep, k[:, lanes]) * SCALE + bias
        raised = jnp.exp(scores - jnp.max(scores, axis=-1, keepdims=True))
        p = raised * (1.0 / jnp.sum(raised, axis=-1, keepdims=True))
        probs[h] = p
        out[:, lanes] += dot(p.astype(BF16), v[:, lanes] * keep)


def attend_back(q, k, v, probs, grad, dq, dk, dv):
    for ref in (dq, dk, dv):
        ref[...] = jnp.zeros_like(ref)
    for h in range(HEADS):
        lanes, keep = span(h)
        o = grad[:, lanes] * keep
        p = probs[h]
        dp = dot_nt(o, v[:, lanes])
        delta = jnp.sum(p * dp, axis=-1, keepdims=True)
        ds = (p * (dp - delta) * SCALE).astype(BF16)
        dq[:, lanes] += dot(ds, k[:, lanes] * keep)
        dk[:, lanes] += dot_tn(ds, q[:, lanes] * keep)
        dv[:, lanes] += dot_tn(p.astype(BF16), o)


def time_bias(time_mask):
    row, frame = iota((ROWS, 32), 0), iota((ROWS, 32), 1)
    spread = ((row >> 2) == frame).astype(F32).astype(BF16)
    mask = (time_mask[...] == 1).astype(F32).astype(BF16)
    mask = dot_nt(dot(spread, mask).astype(BF16), spread)
    a, b = iota((ROWS, ROWS), 0), iota((ROWS, ROWS), 1)
    fa, fb = a >> 2, b >> 2
    ok = ((a & 3) == (b & 3)) & ((fa == fb) | ((fb < fa) & (mask > 0.5)))
    return jnp.where(ok, 0.0, MASKED)


def space_bias(pattern, x):
    slot = iota((1, 256), 1) >> 6
    sides = []
    for row in range(2):
        bias = jnp.zeros((1, 256), F32)
        for r in range(4):
            block = 2 * x - 1 + r
            inside = (block >= 0) & (block < 8)
            seen = (pattern[row, r] == 1) | (r == row + 1)
            value = jnp.where(inside & seen, 0.0, MASKED)
            bias = jnp.where(slot == r, value, bias)
        sides.append(bias)
    return jnp.where(iota((ROWS, 256), 0) < 64, sides[0], sides[1])


def join_qkv(buf, whole):
    def body(i, carry):
        zh, x = i >> 1, (i & 1) * 2
        rows = pl.ds(pl.multiple_of(i * 144, 16), 144)
        pairs = (
            (buf[0, x, zh], buf[0, x + 1, zh], 0),
            (buf[1, zh, x], buf[1, zh, x + 1], 896),
        )
        for a, b, lane in pairs:
            pair = jnp.concatenate([a.reshape(72, 896), b.reshape(72, 896)], axis=0)
            whole[rows, lane : lane + 896] = pair
        return carry

    lax.fori_loop(0, 8, body, 0)


def join_out(buf, space, time):
    def body(zh, carry):
        rows = pl.ds(pl.multiple_of(zh * 144, 16), 144)
        for half in range(2):
            blocks = []
            for x in range(4):
                block = buf[0, x, zh] if half == 0 else buf[1, zh, x]
                blocks.append(block.astype(F32).reshape(72, 640))
            for ref, low in ((space, 0), (time, 36)):
                part = jnp.concatenate([block[low : low + 36] for block in blocks], axis=0)
                ref[rows, half * 640 : half * 640 + 640] = part.astype(BF16)
        return carry

    lax.fori_loop(0, 4, body, 0)


class Total:
    def __init__(self, gather, refs, sems, small):
        self.g = gather
        self.term, self.twin, self.r1, self.u, self.r2, self.v, self.rz, self.vz, self.rl, self.f = refs
        send, recv = sems
        self.small = small
        dp, y, zl, core, x = gather.pos
        term, u, r1, r2 = self.term, self.u, self.r1, self.r2
        self.e2 = Exchange(
            4, gather.p2, gather.along2, lambda i: term.at[core, i], lambda i: r1.at[i], send.at[0], recv.at[0]
        )
        self.e1 = Exchange(
            4, gather.p1, gather.along1, lambda i: u.at[i], lambda i: r2.at[i], send.at[1], recv.at[1]
        )
        self.el = Exchange(
            4,
            zl,
            lambda i: at(dp, y, i, core, x),
            lambda i: self.vz,
            lambda i: self.rl.at[i],
            send.at[2],
            recv.at[2],
        )

    def one(self, slot, src, dst, target, recv_slot=None):
        send, recv = self.small
        return pltpu.make_async_remote_copy(
            src_ref=src,
            dst_ref=dst,
            send_sem=send.at[slot],
            recv_sem=recv.at[slot if recv_slot is None else recv_slot],
            device_id=target,
            device_id_type=MESH,
        )

    def twin_id(self):
        dp, y, zl, core, x = self.g.pos
        return at(dp, y, zl, 1 - core, x)

    def start(self, att, up):
        dp, y, zl, core, x = self.g.pos
        for half in range(2):
            lanes = slice(0, 640) if half == 0 else slice(640, D)
            term = dot_tn(att[:, :WIDTH], up[:, lanes])
            if half == 1:
                term = jnp.concatenate([term, jnp.zeros((WIDTH, 128), F32)], axis=1)
            for s in range(16):
                block = jnp.concatenate([term[36 * s : 36 * s + 36], jnp.zeros((12, 640), F32)], axis=0)
                place = (0, s % 4, s // 4) if half == 0 else (1, s // 4, s % 4)
                self.term[place] = block.astype(BF16)
        self.one(0, self.term.at[1 - core], self.twin, self.twin_id()).start()

    def step1(self):
        dp, y, zl, core, x = self.g.pos
        self.one(0, self.twin, self.twin, self.twin_id()).wait_recv()
        for i in range(4):
            mine = self.term[core, i].astype(F32) + self.twin[i].astype(F32)
            self.term[core, i] = mine.astype(BF16)
        self.e2.start()

    def step2(self):
        dp, y, zl, core, x = self.g.pos
        self.e2.wait()
        p = self.g.p2
        total = self.term[core, p].astype(F32)
        for k in range(1, 4):
            total += self.r1[rem4(p + k)].astype(F32)
        self.u[...] = total.astype(BF16)
        self.e1.start()

    def step3(self):
        dp, y, zl, core, x = self.g.pos
        self.e1.wait()
        p = self.g.p1
        total = self.u[p].astype(F32)
        for k in range(1, 4):
            total += self.r2[rem4(p + k)].astype(F32)
        self.v[...] = total.astype(BF16)

        @pl.when(dp != y)
        def _():
            self.one(1, self.v, self.rz.at[dp], at(y, y, zl, core, x), 1 + rem4(dp - y)).start()

    def step4(self):
        dp, y, zl, core, x = self.g.pos

        @pl.when(dp == y)
        def _():
            total = self.v[...].astype(F32)
            for k in range(1, 4):
                source = rem4(dp + k)
                self.one(1, self.v, self.rz.at[source], self.twin_id(), 1 + k).wait_recv()
                total += self.rz[source].astype(F32)
            self.vz[...] = total.astype(BF16)
            self.el.start()

    def step5(self):
        dp, y, zl, core, x = self.g.pos

        @pl.when(dp == y)
        def _():
            self.el.wait()
            total = self.vz[...].astype(F32)
            for k in range(1, 4):
                total += self.rl[rem4(zl + k)].astype(F32)
            self.f[core] = total.astype(BF16)
            for k in range(1, 4):
                target = at(dp, rem4(y + k), zl, core, x)
                self.one(1 + k, self.f.at[core], self.f.at[core], target, 5).start()

        @pl.when(dp != y)
        def _():
            self.one(2, self.f.at[core], self.f.at[core], self.twin_id(), 5).wait_recv()

        self.one(5, self.f.at[core], self.f.at[core], self.twin_id(), 6).start()

    def step6(self, out):
        dp, y, zl, core, x = self.g.pos
        self.one(5, self.f.at[1 - core], self.f.at[1 - core], self.twin_id(), 6).wait_recv()
        out[:, :640] = self.f[0][:36].astype(F32)
        out[:, 640:] = self.f[1][:36, :512].astype(F32)

    def drain(self):
        dp, y, zl, core, x = self.g.pos
        self.one(0, self.term.at[1 - core], self.twin, self.twin_id()).wait_send()
        self.e2.drain()
        self.e1.drain()

        @pl.when(dp != y)
        def _():
            self.one(1, self.v, self.rz.at[dp], self.twin_id()).wait_send()

        @pl.when(dp == y)
        def _():
            self.el.drain()
            for k in range(1, 4):
                self.one(1 + k, self.f.at[core], self.f.at[core], self.twin_id()).wait_send()

        self.one(5, self.f.at[core], self.f.at[core], self.twin_id()).wait_send()


def halo_copies(low, high, from_low, from_high, sems, slot):
    dp, y, zl, core, x = coords()
    send, recv = sems
    return [
        pltpu.make_async_remote_copy(
            src_ref=src,
            dst_ref=dst,
            send_sem=send.at[slot, i],
            recv_sem=recv.at[slot, i],
            device_id=at(dp, y, zl, core, rem4(x + step)),
            device_id_type=MESH,
        )
        for i, (src, dst, step) in enumerate(((low, from_high, -1), (high, from_low, 1)))
    ]


def kernel(
    latents,
    upstream,
    modulation,
    space_qkv,
    space_out,
    time_qkv,
    time_out,
    pattern,
    time_mask,
    result,
    start_grad,
    out_grad,
    s,
):
    dp, y, zl, core, x = coords()
    gather = Gather((s["g0"], s["g1"], s["g2"]), s["g_send"], s["g_recv"])
    sems = (s["m_send"], s["m_recv"])
    halo_sems = (s["h_send"], s["h_recv"])

    def move(out, name, source, slot):
        return Move(out, source, s[name + "1"], s[name + "2"], s[name + "3"], sems, slot)

    lat_move = move(True, "lat", latents, 0)
    up_move = move(True, "up", upstream, 1)
    att_move = move(True, "att", s["att"], 2)
    back_att = move(False, "batt", s["tatt"], 3)
    back_grad = move(False, "bgrad", s["sgrad"], 4)
    back_mid = move(False, "bmid", s["mid_grad"], 5)
    total = Total(
        gather,
        [s[n] for n in ("term", "twin", "r1", "u", "r2", "v", "rz", "vz", "rl", "f")],
        (s["t_send"], s["t_recv"]),
        (s["o_send"], s["o_recv"]),
    )

    place_own(gather, space_qkv, space_out, time_qkv, time_out)
    greet()
    for g in range(3):
        gather.zsend(g)

    start = latents[...].astype(F32)
    gain_space = 1.0 + modulation[0:1, :]
    gain_time = 1.0 + modulation[1:2, :]
    inverse = inverse_of(start)
    s["inv_s"][...] = inverse
    s["normed"][...] = (start * inverse * gain_space).astype(BF16)
    order = shuffle()
    s["order"][...] = order

    gather.zpass(0)
    gather.s1send(0)
    gather.zpass(1)
    gather.s1pass(0)
    gather.s2send(0)
    gather.zpass(2)
    lat_move.start()
    up_move.start()
    gather.s1send(1)
    gather.s1pass(1)
    gather.s2pass(0)
    gather.s2send(1)
    gather.s1send(2)
    gather.s2done(0)
    gather.s1pass(2)
    gather.end(0)

    join_qkv(s["g0"], s["w0"])
    rows = dot(s["normed"][...], s["w0"][...])
    s["q"][...] = rows[:, :WIDE].astype(BF16)
    s["kv"][0, 64:192] = rows[:, WIDTH : WIDTH + WIDE].astype(BF16)
    s["kv"][1, 64:192] = rows[:, 2 * WIDTH : 2 * WIDTH + WIDE].astype(BF16)
    kv = s["kv"]
    halo = halo_copies(
        kv.at[:, pl.ds(64, 64)],
        kv.at[:, pl.ds(128, 64)],
        kv.at[:, pl.ds(0, 64)],
        kv.at[:, pl.ds(192, 64)],
        halo_sems,
        0,
    )
    for copy in halo:
        copy.start()
    gather.s2pass(1)
    gather.s2send(2)
    lat_move.turn(s["order"][...])
    up_move.turn(s["order"][...])
    bias = space_bias(pattern, x)
    for copy in halo:
        copy.wait_recv()
    attend(s["q"], kv.at[0], kv.at[1], bias, s["probs_s"], s["acc"])
    s["att"][...] = s["acc"][...].astype(BF16)
    att_move.start()
    gather.s2done(1)
    gather.end(1)
    join_out(s["g1"], s["so"], s["to"])
    s["mid_f"][...] = latents[...].astype(F32) + dot(s["att"][:, :WIDTH], s["so"][:, :D])
    att_move.turn(s["order"][...])
    gather.s2pass(2)
    up_move.finish()
    lat_move.finish()
    s["tgrad"][:, :WIDTH] = dot_nt(s["up3"][...], s["to"][:, :D]).astype(BF16)
    s["tgrad"][:, WIDTH:] = jnp.zeros((ROWS, WIDE - WIDTH), BF16)
    s["tbias"][...] = time_bias(time_mask)
    gather.s2done(2)
    gather.end(2)
    join_qkv(s["g2"], s["w2"])
    att_move.finish()

    middle = s["lat3"][...].astype(F32) + dot(s["att3"][:, :WIDTH], s["so"][:, :D])
    inverse = inverse_of(middle)
    s["inv_t"][...] = inverse
    s["mid_p"][...] = middle
    rows = dot((middle * inverse * gain_time).astype(BF16), s["w2"][...])
    s["tq"][...] = rows[:, :WIDE].astype(BF16)
    s["tk"][...] = rows[:, WIDTH : WIDTH + WIDE].astype(BF16)
    s["tv"][...] = rows[:, 2 * WIDTH : 2 * WIDTH + WIDE].astype(BF16)
    attend(s["tq"], s["tk"], s["tv"], s["tbias"][...], s["probs_t"], s["acc"])
    s["tatt"][...] = s["acc"][...].astype(BF16)
    back_att.start()
    total.start(s["tatt"], s["up3"])

    attend_back(s["tq"], s["tk"], s["tv"], s["probs_t"], s["tgrad"], s["acc"], s["tdk"], s["tdv"])
    s["grads"][:, :WIDTH] = s["acc"][:, :WIDTH].astype(BF16)
    s["grads"][:, WIDTH : 2 * WIDTH] = s["tdk"][:, :WIDTH].astype(BF16)
    s["grads"][:, 2 * WIDTH :] = s["tdv"][...].astype(BF16)
    grad = dot_nt(s["grads"][...], s["w2"][...])
    mid_grad = s["up3"][...].astype(F32) + norm_back(s["mid_p"][...], s["inv_t"][...], gain_time, grad)
    s["mid_grad"][...] = mid_grad.astype(BF16)
    s["sgrad"][:, :WIDTH] = dot_nt(s["mid_grad"][...], s["so"][:, :D]).astype(BF16)
    s["sgrad"][:, WIDTH:] = jnp.zeros((ROWS, WIDE - WIDTH), BF16)
    back_grad.start()
    back_mid.start()
    back_att.turn(s["order"][...])
    total.step1()
    back_grad.turn(s["order"][...])
    back_mid.turn(s["order"][...])
    back_att.finish()
    result[...] = (s["mid_f"][...] + dot(s["batt3"][:, :WIDTH], s["to"][:, :D])).astype(BF16)
    total.step2()
    back_grad.finish()

    attend_back(s["q"], kv.at[0], kv.at[1], s["probs_s"], s["bgrad3"], s["acc"], s["dkv"].at[0], s["dkv"].at[1])
    s["rim"][0] = s["dkv"][:, :64].astype(BF16)
    s["rim"][1] = s["dkv"][:, 192:].astype(BF16)
    rim = halo_copies(
        s["rim"].at[0], s["rim"].at[1], s["rim_in"].at[0], s["rim_in"].at[1], halo_sems, 1
    )
    for copy in rim:
        copy.start()
    total.step3()
    grad = dot_nt(s["acc"][...].astype(BF16), s["w0"][:, :WIDE])
    total.step4()
    for copy in rim:
        copy.wait_recv()
    own = s["dkv"][:, 64:192]
    edges = jnp.concatenate([s["rim_in"][0], s["rim_in"][1]], axis=1).astype(F32)
    own = (own + edges).astype(BF16)
    s["grads"][:, WIDTH : 2 * WIDTH] = own[0][:, :WIDTH]
    s["grads"][:, 2 * WIDTH :] = own[1]
    s["grads"][:, 512:WIDTH] = jnp.zeros((ROWS, 64), BF16)
    grad += dot_nt(s["grads"][:, 512:], s["w0"][:, 512:])
    back_mid.finish()
    start = latents[...].astype(F32)
    back = norm_back(start, s["inv_s"][...], gain_space, grad)
    start_grad[...] = (s["bmid3"][...].astype(F32) + back).astype(BF16)
    total.step5()
    total.step6(out_grad)

    for g in range(3):
        gather.drain(g)
    for each in (lat_move, up_move, att_move, back_att, back_grad, back_mid, total):
        each.drain()
    for copy in halo + rim:
        copy.wait_send()


def scratch():
    def vmem(shape, dtype=BF16):
        return pltpu.VMEM(shape, dtype)

    dma = pltpu.SemaphoreType.DMA
    out = {f"g{g}": vmem((2, 4, 4, 9, 8, lanes)) for g, lanes in enumerate(LANES)}
    out.update(g_send=dma((3, 16)), g_recv=dma((3, 16)), m_send=dma((6, 2, 7)), m_recv=dma((6, 2, 7)))
    out.update(h_send=dma((2, 2)), h_recv=dma((2, 2)), t_send=dma((3, 3)), t_recv=dma((3, 3)))
    out.update(o_send=dma((8,)), o_recv=dma((8,)))
    out.update(w0=vmem((D, 1792)), w2=vmem((D, 1792)), so=vmem((WIDTH, 1280)), to=vmem((WIDTH, 1280)))
    for name, lanes in (("lat", D), ("up", D), ("att", WIDE), ("batt", WIDE), ("bgrad", WIDE), ("bmid", D)):
        for leg in range(1, 4):
            out[f"{name}{leg}"] = vmem((ROWS, lanes))
    for name in ("att", "tatt", "sgrad", "q", "tq", "tk", "tv", "tgrad"):
        out[name] = vmem((ROWS, WIDE))
    out.update(normed=vmem((ROWS, D)), mid_grad=vmem((ROWS, D)), order=vmem((ROWS, ROWS)))
    out.update(kv=vmem((2, 256, WIDE)), grads=vmem((ROWS, 1792)))
    out.update(rim=vmem((2, 2, 64, WIDE)), rim_in=vmem((2, 2, 64, WIDE)))
    out.update(inv_s=vmem((ROWS, 1), F32), inv_t=vmem((ROWS, 1), F32), tbias=vmem((ROWS, ROWS), F32))
    out.update(acc=vmem((ROWS, WIDE), F32), tdk=vmem((ROWS, WIDE), F32), tdv=vmem((ROWS, WIDE), F32))
    out.update(dkv=vmem((2, 256, WIDE), F32), mid_f=vmem((ROWS, D), F32), mid_p=vmem((ROWS, D), F32))
    out.update(probs_s=vmem((HEADS, ROWS, 256), F32), probs_t=vmem((HEADS, ROWS, ROWS), F32))
    block = (48, WIDE)
    out.update(term=vmem((2, 4, 4) + block), twin=vmem((4, 4) + block), r1=vmem((4, 4) + block))
    out.update(u=vmem((4,) + block), r2=vmem((4,) + block), v=vmem(block), rz=vmem((4,) + block))
    out.update(vz=vmem(block), rl=vmem((4,) + block), f=vmem((2,) + block))
    return out


def local(
    latents,
    upstream,
    modulation,
    space_qkv,
    space_out,
    time_qkv,
    time_out,
    space_pattern,
    time_mask,
):
    shapes = scratch()
    names = list(shapes)

    def body(*refs):
        kernel(*refs[:12], dict(zip(names, refs[12:])))

    vmem = pl.BlockSpec(memory_space=pltpu.VMEM)
    smem = pl.BlockSpec(memory_space=pltpu.SMEM)
    result, start_grad, out_grad = pl.pallas_call(
        body,
        out_shape=[
            jax.ShapeDtypeStruct((ROWS, D), BF16),
            jax.ShapeDtypeStruct((ROWS, D), BF16),
            jax.ShapeDtypeStruct((36, D), F32),
        ],
        in_specs=[vmem] * 7 + [smem, vmem],
        out_specs=[vmem] * 3,
        scratch_shapes=list(shapes.values()),
        compiler_params=pltpu.CompilerParams(
            collective_id=0, has_side_effects=True, vmem_limit_bytes=60 << 20
        ),
    )(
        latents.reshape(ROWS, D),
        upstream.reshape(ROWS, D),
        modulation.reshape(2, D),
        space_qkv,
        space_out,
        time_qkv,
        time_out,
        space_pattern,
        time_mask,
    )
    return (result.reshape(latents.shape), start_grad.reshape(latents.shape), out_grad)


def solution(mesh):
    in_specs = (
        P("dp", "seq", "tile", None),
        P("dp", "seq", "tile", None),
        P("dp", None, None),
        P(("dp", "tile"), None),
        P(("dp", "tile"), None),
        P(("dp", "tile"), None),
        P(("dp", "tile"), None),
        P("tile", None),
        P(),
    )
    out_specs = (
        P("dp", "seq", "tile", None),
        P("dp", "seq", "tile", None),
        P(("dp", "tile"), None),
    )
    return jax.shard_map(local, mesh=mesh, in_specs=in_specs, out_specs=out_specs, check_vma=False)
```

```python
import jax
import jax.numpy as jnp
from jax import lax
from jax.experimental import pallas as pl
from jax.experimental.pallas import tpu as pltpu
from jax.sharding import PartitionSpec as P

HEADS = 8
HEAD_DIM = 72
WIDTH = HEADS * HEAD_DIM
WIDE = 640
D = 1152
ROWS = 128
EPSILON = 1e-06
MASKED = -1e30
SCALE = HEAD_DIM ** (-0.5)
BF16 = jnp.bfloat16
F32 = jnp.float32

MESH = pl.DeviceIdType.MESH
LANES = (896, 640, 896)


def coords():
    dp, seq, tile = lax.axis_index("dp"), lax.axis_index("seq"), lax.axis_index("tile")
    return dp, seq // 8, (seq // 2) % 4, seq % 2, tile


def at(dp, y, zl, core, tile):
    return (dp, (y * 4 + zl) * 2 + core, tile)


def rem4(value):
    return lax.rem(value + 8, 4)


class Gather:
    def __init__(self, bufs, send, recv):
        self.bufs, self.send, self.recv = bufs, send, recv
        dp, y, zl, core, x = self.pos = coords()
        self.first = core == 0
        self.p1 = jnp.where(self.first, y, x)
        self.p2 = jnp.where(self.first, x, y)
        self.q1 = jnp.where(self.first, x, y)
        self.q2 = jnp.where(self.first, y, x)

    def along1(self, place):
        dp, y, zl, core, x = self.pos
        place = rem4(place)
        return at(dp, jnp.where(self.first, place, y), zl, core, jnp.where(self.first, x, place))

    def along2(self, place):
        dp, y, zl, core, x = self.pos
        place = rem4(place)
        return at(dp, jnp.where(self.first, y, place), zl, core, jnp.where(self.first, place, x))

    def copy(self, g, ref, slot, target=None, recv_slot=None):
        return pltpu.make_async_remote_copy(
            src_ref=ref,
            dst_ref=ref,
            send_sem=self.send.at[g, slot],
            recv_sem=self.recv.at[g, slot if recv_slot is None else recv_slot],
            device_id=at(*self.pos) if target is None else target,
            device_id_type=MESH,
        )

    def block(self, g, i2, i1):
        return self.bufs[g].at[self.pos[3], rem4(i2), rem4(i1)]

    def own(self, g):
        return self.block(g, self.p2, self.p1)

    def third(self, g, t):
        return self.own(g).at[pl.ds(3 * t, 3)]

    def source(self, t):
        return rem4(self.pos[1] - t)

    def zsend(self, g):
        dp, y, zl, core, x = self.pos

        @pl.when((zl < 3) & (dp == self.source(zl)))
        def _():
            for k in range(1, 4):
                self.copy(g, self.third(g, zl), k - 1, at(rem4(dp + k), y, zl, core, x), 0).start()

    def neighbours(self):
        dp, y, zl, core, x = self.pos
        z = dp * 4 + zl
        for i, step in enumerate((1, -1, jnp.where(zl == 2, -2, 2))):
            other = lax.rem(z + step + 16, 16)
            yield i, other // 4, at(other // 4, y, lax.rem(other, 4), core, x)

    def zpass(self, g):
        dp, y, zl, core, x = self.pos

        @pl.when((zl < 3) & (dp != self.source(zl)))
        def _():
            self.copy(g, self.third(g, zl), 0, None, 0).wait_recv()

        for i, their, target in self.neighbours():

            @pl.when((zl < 3) & (their != self.source(zl)))
            def _():
                self.copy(g, self.third(g, zl), 16 + i, target, 1 + zl).start()

    def zdone(self, g):
        dp, y, zl, core, x = self.pos
        for t in range(3):

            @pl.when((dp != self.source(t)) & (zl != t))
            def _():
                self.copy(g, self.third(g, t), 0, None, 1 + t).wait_recv()

    def zend(self, g):
        dp, y, zl, core, x = self.pos

        @pl.when((zl < 3) & (dp == self.source(zl)))
        def _():
            for k in range(3):
                self.copy(g, self.third(g, zl), k).wait_send()

        for i, their, target in self.neighbours():

            @pl.when((zl < 3) & (their != self.source(zl)))
            def _():
                self.copy(g, self.third(g, zl), 16 + i).wait_send()

    def ring(self, g, axis, j, k):
        base = 4 if axis == 1 else 20 + 4 * j
        along, p = (self.along1, self.p1) if axis == 1 else (self.along2, self.p2)
        return base, along, p

    def push(self, g, axis, j=0):
        base, along, p = self.ring(g, axis, j, 0)
        ref = self.block(g, self.p2, self.p1 - j)
        self.copy(g, ref, base, along(p + 1)).start()
        self.copy(g, ref, base + 1, along(p - 1)).start()

    def seen(self, g, axis, j, k):
        return self.block(g, self.p2, self.p1 - k) if axis == 1 else self.block(g, self.p2 - k, self.p1 - j)

    def onward(self, g, axis, j, k):
        base, along, p = self.ring(g, axis, j, k)
        ref = self.seen(g, axis, j, k)
        if k == 1:
            self.copy(g, ref, base).wait_recv()
            self.copy(g, ref.at[pl.ds(0, 5)], base + 2, along(p + 1)).start()
        else:
            self.copy(g, ref, base + 1).wait_recv()
            self.copy(g, ref.at[pl.ds(5, 4)], base + 3, along(p - 1)).start()

    def last(self, g, axis, j):
        base, along, p = self.ring(g, axis, j, 2)
        ref = self.seen(g, axis, j, 2)
        self.copy(g, ref.at[pl.ds(0, 5)], base + 2).wait_recv()
        self.copy(g, ref.at[pl.ds(5, 4)], base + 3).wait_recv()

    def sent(self, g, axis, j):
        base, along, p = self.ring(g, axis, j, 0)
        self.copy(g, self.own(g), base).wait_send()
        self.copy(g, self.own(g), base + 1).wait_send()
        self.copy(g, self.own(g).at[pl.ds(0, 5)], base + 2).wait_send()
        self.copy(g, self.own(g).at[pl.ds(5, 4)], base + 3).wait_send()

    def twin(self, g, k, j):
        dp, y, zl, core, x = self.pos
        ref = self.block(g, self.p2 - k, self.p1 - j)
        self.copy(g, ref, 40 + 4 * j + k, at(dp, y, zl, 1 - core, x)).start()

    def round(self, g, j):
        self.push(g, 2, j)
        self.twin(g, 0, j)

    def open(self, g):
        self.zdone(g)
        self.push(g, 1)
        self.round(g, 0)

    def s1mid(self, g):
        for k in (1, 3):
            self.onward(g, 1, 0, k)
            self.round(g, k)

    def s1end(self, g):
        self.last(g, 1, 0)
        self.round(g, 2)

    def mid(self, g, *rounds):
        for j in rounds:
            for k in (1, 3):
                self.onward(g, 2, j, k)
                self.twin(g, k, j)

    def fin(self, g, *rounds):
        for j in rounds:
            self.last(g, 2, j)
            self.twin(g, 2, j)

    def end(self, g):
        for j in (0, 1, 3, 2):
            for k in (0, 1, 3, 2):
                ref = self.bufs[g].at[1 - self.pos[3], rem4(self.q2 - k), rem4(self.q1 - j)]
                self.copy(g, ref, 40 + 4 * j + k).wait_recv()

    def drain(self, g):
        self.zend(g)
        self.sent(g, 1, 0)
        for j in range(4):
            self.sent(g, 2, j)
            for k in range(4):
                self.copy(g, self.own(g), 40 + 4 * j + k).wait_send()


def greet():
    dp, y, zl, core, x = coords()
    seq = lax.axis_index("seq")
    barrier = pltpu.get_barrier_semaphore()

    def hello(target):
        pl.semaphore_signal(barrier, inc=1, device_id=target, device_id_type=MESH)

    def frame(k, carry):
        hello((dp, lax.rem(seq + k, 32), x))
        return carry

    lax.fori_loop(1, 32, frame, 0)
    for k in range(1, 4):
        hello(at(rem4(dp + k), y, zl, core, x))
        hello(at(dp, y, zl, core, rem4(x + k)))
    for step in (1, 3):
        hello(at(rem4(dp + step), y, 3 - zl, core, x))
    pl.semaphore_wait(barrier, 39)


def place_own(gather, space_qkv, space_out, time_qkv, time_out):
    dp, y, zl, core, x = gather.pos

    def put(g, block):
        block = block.reshape(9, 8, LANES[g])
        for t in range(3):

            @pl.when(dp == gather.source(t))
            def _():
                gather.third(g, t)[...] = block[3 * t : 3 * t + 3]

    for half in range(2):

        @pl.when(core == half)
        def _():
            for g, ref in ((0, space_qkv), (2, time_qkv)):
                if half == 0:
                    block = ref[:, :896]
                else:
                    block = jnp.concatenate([ref[:, 896:], jnp.zeros((72, 64), BF16)], axis=1)
                put(g, block)
            block = jnp.concatenate([space_out[...].astype(F32), time_out[...].astype(F32)], axis=0)
            if half == 0:
                block = block[:, :640]
            else:
                block = jnp.concatenate([block[:, 640:], jnp.zeros((72, 128), F32)], axis=1)
            put(1, block.astype(BF16))


class Exchange:
    def __init__(self, n, me, target, block, slot, send, recv):
        self.n, self.me, self.target = n, me, target
        self.block, self.slot, self.sems = block, slot, (send, recv)

    def copy(self, k, src, dst, target):
        return pltpu.make_async_remote_copy(
            src_ref=src,
            dst_ref=dst,
            send_sem=self.sems[0].at[k - 1],
            recv_sem=self.sems[1].at[k - 1],
            device_id=target,
            device_id_type=MESH,
        )

    def start(self):
        for k in range(1, self.n):
            other = lax.rem(self.me + k, self.n)
            self.copy(k, self.block(other), self.slot(self.me), self.target(other)).start()

    def wait(self):
        for k in range(1, self.n):
            source = lax.rem(self.me + self.n - k, self.n)
            self.copy(k, self.slot(source), self.slot(source), self.target(source)).wait_recv()

    def drain(self):
        for k in range(1, self.n):
            other = lax.rem(self.me + k, self.n)
            self.copy(k, self.block(other), self.slot(self.me), self.target(other)).wait_send()


def dot(a, b):
    return jnp.dot(a, b, preferred_element_type=F32)


def dot_nt(a, b):
    return lax.dot_general(a, b, (((1,), (1,)), ((), ())), preferred_element_type=F32)


def dot_tn(a, b):
    return lax.dot_general(a, b, (((0,), (0,)), ((), ())), preferred_element_type=F32)


def iota(shape, axis):
    return lax.broadcasted_iota(jnp.int32, shape, axis)


class Move:
    def __init__(self, out, source, target, sems, slot):
        self.out, self.source, self.target, self.sems, self.slot = out, source, target, sems, slot
        self.tile, self.dp, self.seq = lax.axis_index("tile"), lax.axis_index("dp"), lax.axis_index("seq")

    def patches(self, seq):
        return (seq & 7) * 4 + (seq >> 3)

    def src(self, other):
        return self.source.at[self.patches(other) if self.out else other]

    def dst(self, owner):
        return self.target.at[owner if self.out else self.patches(owner)]

    def copy(self, k, other, owner):
        send, recv = self.sems
        return pltpu.make_async_remote_copy(
            src_ref=self.src(other),
            dst_ref=self.dst(owner),
            send_sem=send.at[self.slot, k],
            recv_sem=recv.at[self.slot, k],
            device_id=(self.dp, other, self.tile),
            device_id_type=MESH,
        )

    def each(self, step):
        def body(k, carry):
            step(k)
            return carry

        lax.fori_loop(1, 32, body, 0)

    def start(self):
        self.each(lambda k: self.copy(k, lax.rem(self.seq + k, 32), self.seq).start())
        self.dst(self.seq)[...] = self.src(self.seq)[...]

    def finish(self):
        self.each(lambda k: self.copy(k, self.seq, lax.rem(self.seq + 32 - k, 32)).wait_recv())

    def drain(self):
        self.each(lambda k: self.copy(k, self.seq, self.seq).wait_send())


def inverse_of(values):
    return lax.rsqrt(jnp.sum(values * values, axis=-1, keepdims=True) * (1.0 / D) + EPSILON)


def norm_back(values, inverse, gain, grad):
    scaled = grad * gain
    cubed = inverse * inverse * inverse
    mean = jnp.sum(scaled * values, axis=-1, keepdims=True) * (1.0 / D)
    return inverse * scaled - values * (cubed * mean)


def span(h):
    low, high = h * HEAD_DIM, (h + 1) * HEAD_DIM
    begin, end = low // 128 * 128, -(-high // 128) * 128
    lane = iota((1, end - begin), 1) + begin
    keep = ((lane >= low) & (lane < high)).astype(F32).astype(BF16)
    return slice(begin, end), keep


def attend(q, k, v, bias, probs, out):
    out[...] = jnp.zeros_like(out)
    for h in range(HEADS):
        lanes, keep = span(h)
        scores = dot_nt(q[:, lanes] * keep, k[:, lanes]) * SCALE + bias
        raised = jnp.exp(scores - jnp.max(scores, axis=-1, keepdims=True))
        p = raised * (1.0 / jnp.sum(raised, axis=-1, keepdims=True))
        probs[h] = p
        out[:, lanes] += dot(p.astype(BF16), v[:, lanes] * keep)


def attend_back(q, k, v, probs, grad, dq, dk, dv):
    for ref in (dq, dk, dv):
        ref[...] = jnp.zeros_like(ref)
    for h in range(HEADS):
        lanes, keep = span(h)
        o = grad[:, lanes] * keep
        p = probs[h]
        dp = dot_nt(o, v[:, lanes])
        delta = jnp.sum(p * dp, axis=-1, keepdims=True)
        ds = (p * (dp - delta) * SCALE).astype(BF16)
        dq[:, lanes] += dot(ds, k[:, lanes] * keep)
        dk[:, lanes] += dot_tn(ds, q[:, lanes] * keep)
        dv[:, lanes] += dot_tn(p.astype(BF16), o)


def space_back_rim(q, v, probs, grad, ds_all, rim):
    rim[...] = jnp.zeros_like(rim)
    for h in range(HEADS):
        lanes, keep = span(h)
        o = grad[:, lanes] * keep
        p = probs[h]
        dp = dot_nt(o, v[:, lanes])
        delta = jnp.sum(p * dp, axis=-1, keepdims=True)
        ds = (p * (dp - delta) * SCALE).astype(BF16)
        ds_all[h] = ds
        rim[0, :, lanes] += dot_tn(ds[:, 128:], q[:, lanes] * keep)
        rim[1, :, lanes] += dot_tn(p[:, 128:].astype(BF16), o)


def space_back_own(q, k, probs, grad, ds_all, dq, dkv):
    dq[...] = jnp.zeros_like(dq)
    dkv[...] = jnp.zeros_like(dkv)
    for h in range(HEADS):
        lanes, keep = span(h)
        ds = ds_all[h]
        dq[:, lanes] += dot(ds, k[:, lanes] * keep)
        dkv[0, :, lanes] += dot_tn(ds[:, :128], q[:, lanes] * keep)
        dkv[1, :, lanes] += dot_tn(probs[h, :, :128].astype(BF16), grad[:, lanes] * keep)


def time_bias(time_mask):
    row, frame = iota((ROWS, 32), 0), iota((ROWS, 32), 1)
    spread = ((row >> 2) == frame).astype(F32).astype(BF16)
    mask = (time_mask[...] == 1).astype(F32).astype(BF16)
    mask = dot_nt(dot(spread, mask).astype(BF16), spread)
    a, b = iota((ROWS, ROWS), 0), iota((ROWS, ROWS), 1)
    fa, fb = a >> 2, b >> 2
    ok = ((a & 3) == (b & 3)) & ((fa == fb) | ((fb < fa) & (mask > 0.5)))
    return jnp.where(ok, 0.0, MASKED)


def space_bias(pattern, x):
    part = iota((1, 256), 1) >> 6
    slot = jnp.where(part < 2, part + 1, jnp.where(part == 2, 0, 3))
    sides = []
    for row in range(2):
        bias = jnp.zeros((1, 256), F32)
        for r in range(4):
            block = 2 * x - 1 + r
            inside = (block >= 0) & (block < 8)
            seen = (pattern[row, r] == 1) | (r == row + 1)
            value = jnp.where(inside & seen, 0.0, MASKED)
            bias = jnp.where(slot == r, value, bias)
        sides.append(bias)
    return jnp.where(iota((ROWS, 256), 0) < 64, sides[0], sides[1])


def shard(buf, half, zh, x):
    first = half == 0
    parts = []
    for t in range(3):
        share = rem4(zh + t)
        part = buf[half, jnp.where(first, x, share), jnp.where(first, share, x)]
        parts.append(part[3 * t : 3 * t + 3])
    return jnp.concatenate(parts, axis=0).reshape(72, buf.shape[-1])


def join_qkv(buf, whole, half):
    lanes = pl.ds(pl.multiple_of(half * 896, 128), 896)

    def body(i, carry):
        zh, x = i >> 1, (i & 1) * 2
        rows = pl.ds(pl.multiple_of(i * 144, 16), 144)
        pair = jnp.concatenate([shard(buf, half, zh, x), shard(buf, half, zh, x + 1)], axis=0)
        whole[rows, lanes] = pair
        return carry

    lax.fori_loop(0, 8, body, 0)


def join_out(buf, space, time, half):
    lanes = pl.ds(pl.multiple_of(half * 640, 128), 640)

    def body(zh, carry):
        rows = pl.ds(pl.multiple_of(zh * 144, 16), 144)
        blocks = [shard(buf, half, zh, x).astype(F32) for x in range(4)]
        for ref, low in ((space, 0), (time, 36)):
            part = jnp.concatenate([block[low : low + 36] for block in blocks], axis=0)
            ref[rows, lanes] = part.astype(BF16)
        return carry

    lax.fori_loop(0, 4, body, 0)


class Total:
    def __init__(self, gather, refs, sems, small):
        self.g = gather
        self.term, self.r1, self.u, self.r2, self.v, self.ra, self.va, self.rb, self.f = refs
        send, recv = sems
        self.small = small
        dp, y, zl, core, x = gather.pos
        term, u, r1, r2 = self.term, self.u, self.r1, self.r2
        self.e2 = Exchange(
            4, gather.p2, gather.along2, lambda i: term.at[i], lambda i: r1.at[i], send.at[0], recv.at[0]
        )
        self.e1 = Exchange(
            4, gather.p1, gather.along1, lambda i: u.at[i], lambda i: r2.at[i], send.at[1], recv.at[1]
        )

    def one(self, slot, src, dst, target, recv_slot=None):
        send, recv = self.small
        return pltpu.make_async_remote_copy(
            src_ref=src,
            dst_ref=dst,
            send_sem=send.at[slot],
            recv_sem=recv.at[slot if recv_slot is None else recv_slot],
            device_id=target,
            device_id_type=MESH,
        )

    def twin_id(self):
        dp, y, zl, core, x = self.g.pos
        return at(dp, y, zl, 1 - core, x)

    def share(self, up, up2):
        self.one(0, up, up2, self.twin_id()).start()

    def give(self, att, att2):
        self.one(12, att, att2, self.twin_id(), 14).start()

    def step1(self, att, att2, up, up_in, up2):
        dp, y, zl, core, x = self.g.pos
        self.one(0, up_in, up2, self.twin_id()).wait_recv()
        self.one(12, att, att2, self.twin_id(), 14).wait_recv()
        for half in range(2):

            @pl.when(core == half)
            def _():
                lanes = slice(0, 640) if half == 0 else slice(640, D)
                term = dot_tn(att[:, :WIDTH], up[:, lanes])
                term += dot_tn(att2[:, :WIDTH], up2[:, :, lanes].reshape(ROWS, -1))
                if half == 1:
                    term = jnp.concatenate([term, jnp.zeros((WIDTH, 128), F32)], axis=1)
                for i in range(16):
                    block = jnp.concatenate([term[36 * i : 36 * i + 36], jnp.zeros((12, 640), F32)], axis=0)
                    place = (i % 4, i // 4) if half == 0 else (i // 4, i % 4)
                    self.term[place] = block.astype(BF16)

        self.e2.start()

    def step2(self):
        dp, y, zl, core, x = self.g.pos
        self.e2.wait()
        p = self.g.p2
        total = self.term[p].astype(F32)
        for k in range(1, 4):
            total += self.r1[rem4(p + k)].astype(F32)
        self.u[...] = total.astype(BF16)
        self.e1.start()

    def step3(self):
        dp, y, zl, core, x = self.g.pos
        self.e1.wait()
        p = self.g.p1
        total = self.u[p].astype(F32)
        for k in range(1, 4):
            total += self.r2[rem4(p + k)].astype(F32)
        self.v[...] = total.astype(BF16)
        for t in range(3):

            @pl.when(zl != t)
            def _():
                ref = self.v.at[pl.ds(16 * t, 16)]
                self.one(1 + t, ref, self.ra.at[zl], at(dp, y, t, core, x), 1 + zl).start()

    def step4(self):
        dp, y, zl, core, x = self.g.pos

        @pl.when(zl < 3)
        def _():
            total = self.v[pl.ds(pl.multiple_of(16 * zl, 16), 16)].astype(F32)
            for k in range(1, 4):
                source = rem4(zl + k)
                self.one(1, self.ra.at[source], self.ra.at[source], self.twin_id(), 1 + source).wait_recv()
                total += self.ra[source].astype(F32)
            self.va[...] = total.astype(BF16)

            @pl.when(dp != y)
            def _():
                self.one(4, self.va, self.rb.at[dp], at(y, y, zl, core, x), 5 + dp).start()

    def others(self):
        dp, y, zl, core, x = self.g.pos
        for k in range(1, 16):
            chip = lax.rem(y * 4 + zl + k, 16)
            yield k, (dp, chip * 2 + core, x)

    def step5(self):
        dp, y, zl, core, x = self.g.pos

        @pl.when((zl < 3) & (dp == y))
        def _():
            total = self.va[...].astype(F32)
            for k in range(1, 4):
                source = rem4(dp + k)
                self.one(1, self.va, self.rb.at[source], self.twin_id(), 5 + source).wait_recv()
                total += self.rb[source].astype(F32)
            ref = self.f.at[core, pl.ds(pl.multiple_of(16 * zl, 16), 16)]
            ref[...] = total.astype(BF16)
            for k, target in self.others():
                self.one(15 + k, ref, ref, target, 9 + zl).start()

    def step6(self):
        dp, y, zl, core, x = self.g.pos
        whole = self.f.at[core]
        for t in range(3):

            @pl.when((dp != y) | (zl != t))
            def _():
                ref = self.f.at[core, pl.ds(16 * t, 16)]
                self.one(1, ref, ref, self.twin_id(), 9 + t).wait_recv()

        self.one(11, whole, whole, self.twin_id(), 13).start()

    def step7(self, out):
        dp, y, zl, core, x = self.g.pos
        other = self.f.at[1 - core]
        self.one(11, other, other, self.twin_id(), 13).wait_recv()
        out[:, :640] = self.f[0][:36].astype(F32)
        out[:, 640:] = self.f[1][:36, :512].astype(F32)

    def drain(self, att2, up2):
        dp, y, zl, core, x = self.g.pos
        third, whole = self.va, self.f.at[core]
        self.one(0, up2, up2, self.twin_id()).wait_send()
        self.one(12, att2, att2, self.twin_id()).wait_send()
        self.e2.drain()
        self.e1.drain()
        for t in range(3):

            @pl.when(zl != t)
            def _():
                self.one(1 + t, third, third, self.twin_id()).wait_send()

        @pl.when((zl < 3) & (dp != y))
        def _():
            self.one(4, third, third, self.twin_id()).wait_send()

        @pl.when((zl < 3) & (dp == y))
        def _():
            for k in range(1, 16):
                self.one(15 + k, third, third, self.twin_id()).wait_send()

        self.one(11, whole, whole, self.twin_id()).wait_send()


def halo_copies(low, high, from_low, from_high, sems, slot):
    dp, y, zl, core, x = coords()
    send, recv = sems
    return [
        pltpu.make_async_remote_copy(
            src_ref=src,
            dst_ref=dst,
            send_sem=send.at[slot, i],
            recv_sem=recv.at[slot, i],
            device_id=at(dp, y, zl, core, rem4(x + step)),
            device_id_type=MESH,
        )
        for i, (src, dst, step) in enumerate(((low, from_high, -1), (high, from_low, 1)))
    ]


def kernel(
    latents,
    upstream,
    modulation,
    space_qkv,
    space_out,
    time_qkv,
    time_out,
    pattern,
    time_mask,
    result,
    start_grad,
    out_grad,
    s,
):
    dp, y, zl, core, x = coords()
    gather = Gather((s["g0"], s["g1"], s["g2"]), s["g_send"], s["g_recv"])
    sems = (s["m_send"], s["m_recv"])
    halo_sems = (s["h_send"], s["h_recv"])

    def move(out, name, slot):
        return Move(out, s[name + "_out"], s[name + "_in"], sems, slot)

    lat_move = move(True, "lat", 0)
    up_move = move(True, "up", 1)
    att_move = move(True, "att", 2)
    back_att = move(False, "batt", 3)
    back_grad = move(False, "bgrad", 4)
    back_mid = move(False, "bmid", 5)

    def split(name, value):
        s[name + "_out"][...] = value.reshape(32, 4, value.shape[-1])

    def joined(name):
        return s[name + "_in"][...].reshape(ROWS, -1)
    total = Total(
        gather,
        [s[n] for n in ("term", "r1", "u", "r2", "v", "ra", "va", "rb", "f")],
        (s["t_send"], s["t_recv"]),
        (s["o_send"], s["o_recv"]),
    )

    place_own(gather, space_qkv, space_out, time_qkv, time_out)
    greet()
    for g in range(3):
        gather.zsend(g)
    low, high = pl.ds(0, 64), pl.ds(64, 64)
    edge = s["edge"]
    halo = halo_copies(latents.at[low], latents.at[high], edge.at[low], edge.at[high], halo_sems, 0)
    for copy in halo:
        copy.start()

    start = latents[...].astype(F32)
    gain_space = 1.0 + modulation[0:1, :]
    gain_time = 1.0 + modulation[1:2, :]
    inverse = inverse_of(start)
    s["inv_s"][...] = inverse
    s["normed"][:ROWS] = (start * inverse * gain_space).astype(BF16)
    split("lat", latents[...])
    split("up", upstream[...])

    gather.zpass(0)
    gather.open(0)
    gather.zpass(1)
    gather.zpass(2)
    gather.s1mid(0)
    gather.open(1)
    gather.mid(0, 0)
    gather.s1end(0)
    gather.open(2)
    lat_move.start()
    gather.mid(0, 1, 3)
    gather.s1mid(1)
    gather.mid(0, 2)
    up_move.start()
    gather.s1end(1)
    gather.mid(1, 0)
    for copy in halo:
        copy.wait_recv()
    start = edge[...].astype(F32)
    s["normed"][ROWS:] = (start * inverse_of(start) * gain_space).astype(BF16)
    s["sbias"][...] = space_bias(pattern, x)
    s["tbias"][...] = time_bias(time_mask)
    gather.s1mid(2)
    gather.fin(0, 0, 1, 3)
    gather.mid(1, 1, 3)
    gather.s1end(2)
    gather.fin(0, 2)
    gather.mid(2, 0)
    join_qkv(s["g0"], s["w0"], core)
    gather.end(0)
    join_qkv(s["g0"], s["w0"], 1 - core)
    gather.mid(1, 2)
    kv = s["kv"]
    s["q"][...] = dot(s["normed"][:ROWS], s["w0"][:, :WIDE]).astype(BF16)
    rows = dot(s["normed"][...], s["w0"][:, 512:])
    kv[0] = rows[:, 64 : 64 + WIDE].astype(BF16)
    kv[1] = rows[:, WIDE : 2 * WIDE].astype(BF16)
    gather.mid(2, 1, 3)
    attend(s["q"], kv.at[0], kv.at[1], s["sbias"][...], s["probs_s"], s["acc"])
    att = s["acc"][...].astype(BF16)
    split("att", att)
    att_move.start()
    gather.mid(2, 2)
    gather.fin(1, 0, 1, 3, 2)
    join_out(s["g1"], s["so"], s["to"], core)
    gather.end(1)
    join_out(s["g1"], s["so"], s["to"], 1 - core)
    gather.fin(2, 0, 1, 3)
    s["mid_f"][...] = latents[...].astype(F32) + dot(att[:, :WIDTH], s["so"][:, :D])
    gather.fin(2, 2)
    up_move.finish()
    total.share(s["up_in"], s["up2"])
    s["up"][...] = joined("up")
    s["tgrad"][:, :WIDTH] = dot_nt(s["up"][...], s["to"][:, :D]).astype(BF16)
    s["tgrad"][:, WIDTH:] = jnp.zeros((ROWS, WIDE - WIDTH), BF16)
    lat_move.finish()
    att_move.finish()

    middle = joined("lat").astype(F32) + dot(joined("att")[:, :WIDTH], s["so"][:, :D])
    inverse = inverse_of(middle)
    s["inv_t"][...] = inverse
    s["mid_p"][...] = middle
    join_qkv(s["g2"], s["w2"], core)
    gather.end(2)
    join_qkv(s["g2"], s["w2"], 1 - core)
    rows = dot((middle * inverse * gain_time).astype(BF16), s["w2"][...])
    s["tq"][...] = rows[:, :WIDE].astype(BF16)
    s["tk"][...] = rows[:, WIDTH : WIDTH + WIDE].astype(BF16)
    s["tv"][...] = rows[:, 2 * WIDTH : 2 * WIDTH + WIDE].astype(BF16)
    attend(s["tq"], s["tk"], s["tv"], s["tbias"][...], s["probs_t"], s["acc"])
    s["tatt"][...] = s["acc"][...].astype(BF16)
    total.give(s["tatt"], s["tatt2"])
    split("batt", s["tatt"][...])

    attend_back(s["tq"], s["tk"], s["tv"], s["probs_t"], s["tgrad"], s["acc"], s["tdk"], s["tdv"])
    s["grads"][:, :WIDTH] = s["acc"][:, :WIDTH].astype(BF16)
    s["grads"][:, WIDTH : 2 * WIDTH] = s["tdk"][:, :WIDTH].astype(BF16)
    s["grads"][:, 2 * WIDTH :] = s["tdv"][...].astype(BF16)
    total.step1(s["tatt"], s["tatt2"], s["up"], s["up_in"], s["up2"])
    grad = dot_nt(s["grads"][...], s["w2"][...])
    mid_grad = s["up"][...].astype(F32) + norm_back(s["mid_p"][...], s["inv_t"][...], gain_time, grad)
    s["mid_grad"][...] = mid_grad.astype(BF16)
    s["sgrad"][:, :WIDTH] = dot_nt(s["mid_grad"][...], s["so"][:, :D]).astype(BF16)
    s["sgrad"][:, WIDTH:] = jnp.zeros((ROWS, WIDE - WIDTH), BF16)
    split("bgrad", s["sgrad"][...])
    back_grad.start()
    back_att.start()
    split("bmid", s["mid_grad"][...])
    back_mid.start()
    total.step2()
    total.step3()
    back_grad.finish()
    s["sgrad"][...] = joined("bgrad")

    space_back_rim(s["q"], kv.at[1], s["probs_s"], s["sgrad"], s["ds"], s["rim32"])
    s["rim"][...] = s["rim32"][...].astype(BF16)
    out_rim, in_rim = s["rim"], s["rim_in"]
    rim = halo_copies(
        out_rim.at[:, low], out_rim.at[:, high], in_rim.at[:, low], in_rim.at[:, high], halo_sems, 1
    )
    for copy in rim:
        copy.start()
    total.step4()
    space_back_own(s["q"], kv.at[0], s["probs_s"], s["sgrad"], s["ds"], s["acc"], s["dkv"])
    grad = dot_nt(s["acc"][...].astype(BF16), s["w0"][:, :WIDE])
    total.step5()
    back_att.finish()
    result[...] = (s["mid_f"][...] + dot(joined("batt")[:, :WIDTH], s["to"][:, :D])).astype(BF16)
    for copy in rim:
        copy.wait_recv()
    own = (s["dkv"][...] + in_rim[...].astype(F32)).astype(BF16)
    s["grads"][:, WIDTH : 2 * WIDTH] = own[0][:, :WIDTH]
    s["grads"][:, 2 * WIDTH :] = own[1]
    s["grads"][:, 512:WIDTH] = jnp.zeros((ROWS, 64), BF16)
    grad += dot_nt(s["grads"][:, 512:], s["w0"][:, 512:])
    back_mid.finish()
    start = latents[...].astype(F32)
    back = norm_back(start, s["inv_s"][...], gain_space, grad)
    start_grad[...] = (joined("bmid").astype(F32) + back).astype(BF16)
    total.step6()
    total.step7(out_grad)

    for g in range(3):
        gather.drain(g)
    for each in (lat_move, up_move, att_move, back_att, back_grad, back_mid):
        each.drain()
    total.drain(s["tatt2"], s["up2"])
    for copy in halo + rim:
        copy.wait_send()


def scratch():
    def vmem(shape, dtype=BF16):
        return pltpu.VMEM(shape, dtype)

    dma = pltpu.SemaphoreType.DMA
    out = {f"g{g}": vmem((2, 4, 4, 9, 8, lanes)) for g, lanes in enumerate(LANES)}
    out.update(g_send=dma((3, 56)), g_recv=dma((3, 56)), m_send=dma((6, 32)), m_recv=dma((6, 32)))
    out.update(h_send=dma((2, 2)), h_recv=dma((2, 2)), t_send=dma((2, 3)), t_recv=dma((2, 3)))
    out.update(o_send=dma((32,)), o_recv=dma((16,)))
    out.update(w0=vmem((D, 1792)), w2=vmem((D, 1792)), so=vmem((WIDTH, 1280)), to=vmem((WIDTH, 1280)))
    for name, lanes in (("lat", D), ("up", D), ("att", WIDE), ("batt", WIDE), ("bgrad", WIDE), ("bmid", D)):
        out[name + "_out"], out[name + "_in"] = vmem((32, 4, lanes)), vmem((32, 4, lanes))
    for name in ("tatt", "tatt2", "q", "tq", "tk", "tv", "tgrad", "sgrad"):
        out[name] = vmem((ROWS, WIDE))
    out.update(normed=vmem((256, D)), mid_grad=vmem((ROWS, D)), up=vmem((ROWS, D)), up2=vmem((32, 4, D)))
    out.update(kv=vmem((2, 256, WIDE)), grads=vmem((ROWS, 1792)))
    out.update(rim=vmem((2, ROWS, WIDE)), rim_in=vmem((2, ROWS, WIDE)), edge=vmem((ROWS, D)))
    out.update(inv_s=vmem((ROWS, 1), F32), inv_t=vmem((ROWS, 1), F32), tbias=vmem((ROWS, ROWS), F32), sbias=vmem((ROWS, 256), F32))
    out.update(acc=vmem((ROWS, WIDE), F32), tdk=vmem((ROWS, WIDE), F32), tdv=vmem((ROWS, WIDE), F32))
    out.update(dkv=vmem((2, ROWS, WIDE), F32), rim32=vmem((2, ROWS, WIDE), F32), ds=vmem((HEADS, ROWS, 256)), mid_f=vmem((ROWS, D), F32), mid_p=vmem((ROWS, D), F32))
    out.update(probs_s=vmem((HEADS, ROWS, 256), F32), probs_t=vmem((HEADS, ROWS, ROWS), F32))
    block = (48, WIDE)
    out.update(term=vmem((4, 4) + block), r1=vmem((4, 4) + block))
    out.update(u=vmem((4,) + block), r2=vmem((4,) + block), v=vmem(block), ra=vmem((4, 16, WIDE)))
    out.update(va=vmem((16, WIDE)), rb=vmem((4, 16, WIDE)), f=vmem((2,) + block))
    return out


def local(
    latents,
    upstream,
    modulation,
    space_qkv,
    space_out,
    time_qkv,
    time_out,
    space_pattern,
    time_mask,
):
    shapes = scratch()
    names = list(shapes)

    def body(*refs):
        kernel(*refs[:12], dict(zip(names, refs[12:])))

    vmem = pl.BlockSpec(memory_space=pltpu.VMEM)
    smem = pl.BlockSpec(memory_space=pltpu.SMEM)
    result, start_grad, out_grad = pl.pallas_call(
        body,
        out_shape=[
            jax.ShapeDtypeStruct((ROWS, D), BF16),
            jax.ShapeDtypeStruct((ROWS, D), BF16),
            jax.ShapeDtypeStruct((36, D), F32),
        ],
        in_specs=[vmem] * 7 + [smem, vmem],
        out_specs=[vmem] * 3,
        scratch_shapes=list(shapes.values()),
        compiler_params=pltpu.CompilerParams(
            collective_id=0, has_side_effects=True, vmem_limit_bytes=60 << 20
        ),
    )(
        latents.reshape(ROWS, D),
        upstream.reshape(ROWS, D),
        modulation.reshape(2, D),
        space_qkv,
        space_out,
        time_qkv,
        time_out,
        space_pattern,
        time_mask,
    )
    return (result.reshape(latents.shape), start_grad.reshape(latents.shape), out_grad)


def solution(mesh):
    in_specs = (
        P("dp", "seq", "tile", None),
        P("dp", "seq", "tile", None),
        P("dp", None, None),
        P(("dp", "tile"), None),
        P(("dp", "tile"), None),
        P(("dp", "tile"), None),
        P(("dp", "tile"), None),
        P("tile", None),
        P(),
    )
    out_specs = (
        P("dp", "seq", "tile", None),
        P("dp", "seq", "tile", None),
        P(("dp", "tile"), None),
    )
    return jax.shard_map(local, mesh=mesh, in_specs=in_specs, out_specs=out_specs, check_vma=False)
```

```python
import jax
import jax.numpy as jnp
from jax import lax
from jax.experimental import pallas as pl
from jax.experimental.pallas import tpu as pltpu
from jax.sharding import PartitionSpec as P

HEADS = 8
HEAD_DIM = 72
WIDTH = HEADS * HEAD_DIM
WIDE = 640
D = 1152
ROWS = 128
EPSILON = 1e-06
MASKED = -1e30
SCALE = HEAD_DIM ** (-0.5)
BF16 = jnp.bfloat16
F32 = jnp.float32

MESH = pl.DeviceIdType.MESH
LANES = (896, 640, 896)


def coords():
    dp, seq, tile = lax.axis_index("dp"), lax.axis_index("seq"), lax.axis_index("tile")
    return dp, seq // 8, (seq // 2) % 4, seq % 2, tile


def at(dp, y, zl, core, tile):
    return (dp, (y * 4 + zl) * 2 + core, tile)


def rem4(value):
    return lax.rem(value + 8, 4)


class Gather:
    def __init__(self, bufs, send, recv):
        self.bufs, self.send, self.recv = bufs, send, recv
        dp, y, zl, core, x = self.pos = coords()
        self.first = core == 0
        self.p1 = jnp.where(self.first, y, x)
        self.p2 = jnp.where(self.first, x, y)
        self.q1 = jnp.where(self.first, x, y)
        self.q2 = jnp.where(self.first, y, x)

    def along1(self, place):
        dp, y, zl, core, x = self.pos
        place = rem4(place)
        return at(dp, jnp.where(self.first, place, y), zl, core, jnp.where(self.first, x, place))

    def along2(self, place):
        dp, y, zl, core, x = self.pos
        place = rem4(place)
        return at(dp, jnp.where(self.first, y, place), zl, core, jnp.where(self.first, place, x))

    def copy(self, g, ref, slot, target=None, recv_slot=None):
        return pltpu.make_async_remote_copy(
            src_ref=ref,
            dst_ref=ref,
            send_sem=self.send.at[g, slot],
            recv_sem=self.recv.at[g, slot if recv_slot is None else recv_slot],
            device_id=at(*self.pos) if target is None else target,
            device_id_type=MESH,
        )

    def block(self, g, i2, i1):
        return self.bufs[g].at[self.pos[3], rem4(i2), rem4(i1)]

    def own(self, g):
        return self.block(g, self.p2, self.p1)

    def third(self, g, t):
        return self.own(g).at[pl.ds(3 * t, 3)]

    def source(self, t):
        return rem4(self.pos[1] - t)

    def zsend(self, g):
        dp, y, zl, core, x = self.pos

        @pl.when((zl < 3) & (dp == self.source(zl)))
        def _():
            for k in range(1, 4):
                self.copy(g, self.third(g, zl), k - 1, at(rem4(dp + k), y, zl, core, x), 0).start()

    def neighbours(self):
        dp, y, zl, core, x = self.pos
        z = dp * 4 + zl
        for i, step in enumerate((1, -1, jnp.where(zl == 2, -2, 2))):
            other = lax.rem(z + step + 16, 16)
            yield i, other // 4, at(other // 4, y, lax.rem(other, 4), core, x)

    def zpass(self, g):
        dp, y, zl, core, x = self.pos

        @pl.when((zl < 3) & (dp != self.source(zl)))
        def _():
            self.copy(g, self.third(g, zl), 0, None, 0).wait_recv()

        for i, their, target in self.neighbours():

            @pl.when((zl < 3) & (their != self.source(zl)))
            def _():
                self.copy(g, self.third(g, zl), 16 + i, target, 1 + zl).start()

    def zdone(self, g):
        dp, y, zl, core, x = self.pos
        for t in range(3):

            @pl.when((dp != self.source(t)) & (zl != t))
            def _():
                self.copy(g, self.third(g, t), 0, None, 1 + t).wait_recv()

    def zend(self, g):
        dp, y, zl, core, x = self.pos

        @pl.when((zl < 3) & (dp == self.source(zl)))
        def _():
            for k in range(3):
                self.copy(g, self.third(g, zl), k).wait_send()

        for i, their, target in self.neighbours():

            @pl.when((zl < 3) & (their != self.source(zl)))
            def _():
                self.copy(g, self.third(g, zl), 16 + i).wait_send()

    def ring(self, g, axis, j, k):
        base = 4 if axis == 1 else 20 + 4 * j
        along, p = (self.along1, self.p1) if axis == 1 else (self.along2, self.p2)
        return base, along, p

    def push(self, g, axis, j=0):
        base, along, p = self.ring(g, axis, j, 0)
        ref = self.block(g, self.p2, self.p1 - j)
        self.copy(g, ref, base, along(p + 1)).start()
        self.copy(g, ref, base + 1, along(p - 1)).start()

    def seen(self, g, axis, j, k):
        return self.block(g, self.p2, self.p1 - k) if axis == 1 else self.block(g, self.p2 - k, self.p1 - j)

    def onward(self, g, axis, j, k):
        base, along, p = self.ring(g, axis, j, k)
        ref = self.seen(g, axis, j, k)
        if k == 1:
            self.copy(g, ref, base).wait_recv()
            self.copy(g, ref.at[pl.ds(0, 5)], base + 2, along(p + 1)).start()
        else:
            self.copy(g, ref, base + 1).wait_recv()
            self.copy(g, ref.at[pl.ds(5, 4)], base + 3, along(p - 1)).start()

    def last(self, g, axis, j):
        base, along, p = self.ring(g, axis, j, 2)
        ref = self.seen(g, axis, j, 2)
        self.copy(g, ref.at[pl.ds(0, 5)], base + 2).wait_recv()
        self.copy(g, ref.at[pl.ds(5, 4)], base + 3).wait_recv()

    def sent(self, g, axis, j):
        base, along, p = self.ring(g, axis, j, 0)
        self.copy(g, self.own(g), base).wait_send()
        self.copy(g, self.own(g), base + 1).wait_send()
        self.copy(g, self.own(g).at[pl.ds(0, 5)], base + 2).wait_send()
        self.copy(g, self.own(g).at[pl.ds(5, 4)], base + 3).wait_send()

    def twin(self, g, k, j):
        dp, y, zl, core, x = self.pos
        ref = self.block(g, self.p2 - k, self.p1 - j)
        self.copy(g, ref, 40 + 4 * j + k, at(dp, y, zl, 1 - core, x)).start()

    def round(self, g, j):
        self.push(g, 2, j)
        self.twin(g, 0, j)

    def open(self, g):
        self.zdone(g)
        self.push(g, 1)
        self.round(g, 0)

    def s1mid(self, g):
        for k in (1, 3):
            self.onward(g, 1, 0, k)
            self.round(g, k)

    def s1end(self, g):
        self.last(g, 1, 0)
        self.round(g, 2)

    def mid(self, g, *rounds):
        for j in rounds:
            for k in (1, 3):
                self.onward(g, 2, j, k)
                self.twin(g, k, j)

    def fin(self, g, *rounds):
        for j in rounds:
            self.last(g, 2, j)
            self.twin(g, 2, j)

    def end(self, g):
        for j in (0, 1, 3, 2):
            for k in (0, 1, 3, 2):
                ref = self.bufs[g].at[1 - self.pos[3], rem4(self.q2 - k), rem4(self.q1 - j)]
                self.copy(g, ref, 40 + 4 * j + k).wait_recv()

    def drain(self, g):
        self.zend(g)
        self.sent(g, 1, 0)
        for j in range(4):
            self.sent(g, 2, j)
            for k in range(4):
                self.copy(g, self.own(g), 40 + 4 * j + k).wait_send()


def greet():
    dp, y, zl, core, x = coords()
    seq = lax.axis_index("seq")
    barrier = pltpu.get_barrier_semaphore()

    def hello(target):
        pl.semaphore_signal(barrier, inc=1, device_id=target, device_id_type=MESH)

    def frame(k, carry):
        hello((dp, lax.rem(seq + k, 32), x))
        return carry

    lax.fori_loop(1, 32, frame, 0)
    for k in range(1, 4):
        hello(at(rem4(dp + k), y, zl, core, x))
        hello(at(dp, y, zl, core, rem4(x + k)))
    for step in (1, 3):
        hello(at(rem4(dp + step), y, 3 - zl, core, x))
    pl.semaphore_wait(barrier, 39)


def place_own(gather, space_qkv, space_out, time_qkv, time_out):
    dp, y, zl, core, x = gather.pos

    def put(g, block):
        block = block.reshape(9, 8, LANES[g])
        for t in range(3):

            @pl.when(dp == gather.source(t))
            def _():
                gather.third(g, t)[...] = block[3 * t : 3 * t + 3]

    for half in range(2):

        @pl.when(core == half)
        def _():
            for g, ref in ((0, space_qkv), (2, time_qkv)):
                if half == 0:
                    block = ref[:, :896]
                else:
                    block = jnp.concatenate([ref[:, 896:], jnp.zeros((72, 64), BF16)], axis=1)
                put(g, block)
            block = jnp.concatenate([space_out[...].astype(F32), time_out[...].astype(F32)], axis=0)
            if half == 0:
                block = block[:, :640]
            else:
                block = jnp.concatenate([block[:, 640:], jnp.zeros((72, 128), F32)], axis=1)
            put(1, block.astype(BF16))


class Exchange:
    def __init__(self, n, me, target, block, slot, send, recv):
        self.n, self.me, self.target = n, me, target
        self.block, self.slot, self.sems = block, slot, (send, recv)

    def copy(self, k, src, dst, target):
        return pltpu.make_async_remote_copy(
            src_ref=src,
            dst_ref=dst,
            send_sem=self.sems[0].at[k - 1],
            recv_sem=self.sems[1].at[k - 1],
            device_id=target,
            device_id_type=MESH,
        )

    def start(self):
        for k in range(1, self.n):
            other = lax.rem(self.me + k, self.n)
            self.copy(k, self.block(other), self.slot(self.me), self.target(other)).start()

    def wait(self):
        for k in range(1, self.n):
            source = lax.rem(self.me + self.n - k, self.n)
            self.copy(k, self.slot(source), self.slot(source), self.target(source)).wait_recv()

    def drain(self):
        for k in range(1, self.n):
            other = lax.rem(self.me + k, self.n)
            self.copy(k, self.block(other), self.slot(self.me), self.target(other)).wait_send()


def dot(a, b):
    return jnp.dot(a, b, preferred_element_type=F32)


def dot_nt(a, b):
    return lax.dot_general(a, b, (((1,), (1,)), ((), ())), preferred_element_type=F32)


def dot_tn(a, b):
    return lax.dot_general(a, b, (((0,), (0,)), ((), ())), preferred_element_type=F32)


def iota(shape, axis):
    return lax.broadcasted_iota(jnp.int32, shape, axis)


class Move:
    def __init__(self, out, source, target, sems, slot):
        self.out, self.source, self.target, self.sems, self.slot = out, source, target, sems, slot
        self.tile, self.dp, self.seq = lax.axis_index("tile"), lax.axis_index("dp"), lax.axis_index("seq")

    def patches(self, seq):
        return (seq & 7) * 4 + (seq >> 3)

    def src(self, other):
        return self.source.at[self.patches(other) if self.out else other]

    def dst(self, owner):
        return self.target.at[owner if self.out else self.patches(owner)]

    def copy(self, k, other, owner):
        send, recv = self.sems
        return pltpu.make_async_remote_copy(
            src_ref=self.src(other),
            dst_ref=self.dst(owner),
            send_sem=send.at[self.slot, k],
            recv_sem=recv.at[self.slot, k],
            device_id=(self.dp, other, self.tile),
            device_id_type=MESH,
        )

    def each(self, step):
        def body(k, carry):
            step(k)
            return carry

        lax.fori_loop(1, 32, body, 0)

    def start(self):
        self.each(lambda k: self.copy(k, lax.rem(self.seq + k, 32), self.seq).start())
        self.dst(self.seq)[...] = self.src(self.seq)[...]

    def finish(self):
        self.each(lambda k: self.copy(k, self.seq, lax.rem(self.seq + 32 - k, 32)).wait_recv())

    def drain(self):
        self.each(lambda k: self.copy(k, self.seq, self.seq).wait_send())


def inverse_of(values):
    return lax.rsqrt(jnp.sum(values * values, axis=-1, keepdims=True) * (1.0 / D) + EPSILON)


def norm_back(values, inverse, gain, grad):
    scaled = grad * gain
    cubed = inverse * inverse * inverse
    mean = jnp.sum(scaled * values, axis=-1, keepdims=True) * (1.0 / D)
    return inverse * scaled - values * (cubed * mean)


def span(h):
    low, high = h * HEAD_DIM, (h + 1) * HEAD_DIM
    begin, end = low // 128 * 128, -(-high // 128) * 128
    lane = iota((1, end - begin), 1) + begin
    keep = ((lane >= low) & (lane < high)).astype(F32).astype(BF16)
    return slice(begin, end), keep


def attend(q, k, v, bias, probs, out):
    out[...] = jnp.zeros_like(out)
    for h in range(HEADS):
        lanes, keep = span(h)
        scores = dot_nt(q[:, lanes] * keep, k[:, lanes]) * SCALE + bias
        raised = jnp.exp(scores - jnp.max(scores, axis=-1, keepdims=True))
        p = raised * (1.0 / jnp.sum(raised, axis=-1, keepdims=True))
        probs[h] = p
        out[:, lanes] += dot(p.astype(BF16), v[:, lanes] * keep)


def attend_back(q, k, v, probs, grad, dq, dk, dv):
    for ref in (dq, dk, dv):
        ref[...] = jnp.zeros_like(ref)
    for h in range(HEADS):
        lanes, keep = span(h)
        o = grad[:, lanes] * keep
        p = probs[h]
        dp = dot_nt(o, v[:, lanes])
        delta = jnp.sum(p * dp, axis=-1, keepdims=True)
        ds = (p * (dp - delta) * SCALE).astype(BF16)
        dq[:, lanes] += dot(ds, k[:, lanes] * keep)
        dk[:, lanes] += dot_tn(ds, q[:, lanes] * keep)
        dv[:, lanes] += dot_tn(p.astype(BF16), o)


def space_back_rim(q, v, probs, grad, ds_all, rim):
    rim[...] = jnp.zeros_like(rim)
    for h in range(HEADS):
        lanes, keep = span(h)
        o = grad[:, lanes] * keep
        p = probs[h]
        dp = dot_nt(o, v[:, lanes])
        delta = jnp.sum(p * dp, axis=-1, keepdims=True)
        ds = (p * (dp - delta) * SCALE).astype(BF16)
        ds_all[h] = ds
        rim[0, :, lanes] += dot_tn(ds[:, 128:], q[:, lanes] * keep)
        rim[1, :, lanes] += dot_tn(p[:, 128:].astype(BF16), o)


def space_back_own(q, k, probs, grad, ds_all, dq, dkv):
    dq[...] = jnp.zeros_like(dq)
    dkv[...] = jnp.zeros_like(dkv)
    for h in range(HEADS):
        lanes, keep = span(h)
        ds = ds_all[h]
        dq[:, lanes] += dot(ds, k[:, lanes] * keep)
        dkv[0, :, lanes] += dot_tn(ds[:, :128], q[:, lanes] * keep)
        dkv[1, :, lanes] += dot_tn(probs[h, :, :128].astype(BF16), grad[:, lanes] * keep)


def time_bias(time_mask):
    row, frame = iota((ROWS, 32), 0), iota((ROWS, 32), 1)
    spread = ((row >> 2) == frame).astype(F32).astype(BF16)
    mask = (time_mask[...] == 1).astype(F32).astype(BF16)
    mask = dot_nt(dot(spread, mask).astype(BF16), spread)
    a, b = iota((ROWS, ROWS), 0), iota((ROWS, ROWS), 1)
    fa, fb = a >> 2, b >> 2
    ok = ((a & 3) == (b & 3)) & ((fa == fb) | ((fb < fa) & (mask > 0.5)))
    return jnp.where(ok, 0.0, MASKED)


def space_bias(pattern, x):
    part = iota((1, 256), 1) >> 6
    slot = jnp.where(part < 2, part + 1, jnp.where(part == 2, 0, 3))
    sides = []
    for row in range(2):
        bias = jnp.zeros((1, 256), F32)
        for r in range(4):
            block = 2 * x - 1 + r
            inside = (block >= 0) & (block < 8)
            seen = (pattern[row, r] == 1) | (r == row + 1)
            value = jnp.where(inside & seen, 0.0, MASKED)
            bias = jnp.where(slot == r, value, bias)
        sides.append(bias)
    return jnp.where(iota((ROWS, 256), 0) < 64, sides[0], sides[1])


def shard(buf, half, zh, x):
    first = half == 0
    parts = []
    for t in range(3):
        share = rem4(zh + t)
        part = buf[half, jnp.where(first, x, share), jnp.where(first, share, x)]
        parts.append(part[3 * t : 3 * t + 3])
    return jnp.concatenate(parts, axis=0).reshape(72, buf.shape[-1])


def join_qkv(buf, whole, half):
    lanes = pl.ds(pl.multiple_of(half * 896, 128), 896)

    def body(i, carry):
        zh, x = i >> 1, (i & 1) * 2
        rows = pl.ds(pl.multiple_of(i * 144, 16), 144)
        pair = jnp.concatenate([shard(buf, half, zh, x), shard(buf, half, zh, x + 1)], axis=0)
        whole[rows, lanes] = pair
        return carry

    lax.fori_loop(0, 8, body, 0)


def join_out(buf, space, time, half):
    lanes = pl.ds(pl.multiple_of(half * 640, 128), 640)

    def body(zh, carry):
        rows = pl.ds(pl.multiple_of(zh * 144, 16), 144)
        blocks = [shard(buf, half, zh, x).astype(F32) for x in range(4)]
        for ref, low in ((space, 0), (time, 36)):
            part = jnp.concatenate([block[low : low + 36] for block in blocks], axis=0)
            ref[rows, lanes] = part.astype(BF16)
        return carry

    lax.fori_loop(0, 4, body, 0)


class Total:
    def __init__(self, gather, refs, sems, small):
        self.g = gather
        self.term, self.r1, self.u, self.r2, self.v, self.ra, self.va, self.rb, self.f = refs
        send, recv = sems
        self.small = small
        dp, y, zl, core, x = gather.pos
        term, u, r1, r2 = self.term, self.u, self.r1, self.r2
        self.e2 = Exchange(
            4, gather.p2, gather.along2, lambda i: term.at[i], lambda i: r1.at[i], send.at[0], recv.at[0]
        )
        self.e1 = Exchange(
            4, gather.p1, gather.along1, lambda i: u.at[i], lambda i: r2.at[i], send.at[1], recv.at[1]
        )

    def one(self, slot, src, dst, target, recv_slot=None):
        send, recv = self.small
        return pltpu.make_async_remote_copy(
            src_ref=src,
            dst_ref=dst,
            send_sem=send.at[slot],
            recv_sem=recv.at[slot if recv_slot is None else recv_slot],
            device_id=target,
            device_id_type=MESH,
        )

    def twin_id(self):
        dp, y, zl, core, x = self.g.pos
        return at(dp, y, zl, 1 - core, x)

    def share(self, up, up2):
        self.one(0, up, up2, self.twin_id()).start()

    def give(self, att, att2):
        self.one(12, att, att2, self.twin_id(), 14).start()

    def step1(self, att, att2, up, up_in, up2):
        dp, y, zl, core, x = self.g.pos
        for half in range(2):

            @pl.when(core == half)
            def _():
                lanes = slice(0, 640) if half == 0 else slice(640, D)
                term = dot_tn(att[:, :WIDTH], up[:, lanes])
                self.one(0, up_in, up2, self.twin_id()).wait_recv()
                self.one(12, att, att2, self.twin_id(), 14).wait_recv()
                term += dot_tn(att2[:, :WIDTH], up2[:, :, lanes].reshape(ROWS, -1))
                if half == 1:
                    term = jnp.concatenate([term, jnp.zeros((WIDTH, 128), F32)], axis=1)
                for i in range(4):
                    if half == 0:
                        rows = [term[36 * (4 * j + i) : 36 * (4 * j + i) + 36] for j in range(4)]
                        self.term[i] = jnp.concatenate(rows, axis=0).astype(BF16)
                    else:
                        self.term[i] = term[144 * i : 144 * i + 144].astype(BF16)

        self.e2.start()

    def step2(self):
        dp, y, zl, core, x = self.g.pos
        self.e2.wait()
        p = self.g.p2
        total = self.term[p].astype(F32)
        for k in range(1, 4):
            total += self.r1[rem4(p + k)].astype(F32)
        for i in range(4):
            block = jnp.concatenate([total[36 * i : 36 * i + 36], jnp.zeros((12, 640), F32)], axis=0)
            self.u[i] = block.astype(BF16)
        self.e1.start()

    def step3(self):
        dp, y, zl, core, x = self.g.pos
        self.e1.wait()
        p = self.g.p1
        total = self.u[p].astype(F32)
        for k in range(1, 4):
            total += self.r2[rem4(p + k)].astype(F32)
        self.v[...] = total.astype(BF16)
        for t in range(3):

            @pl.when(zl != t)
            def _():
                ref = self.v.at[pl.ds(16 * t, 16)]
                self.one(1 + t, ref, self.ra.at[zl], at(dp, y, t, core, x), 1 + zl).start()

    def step4(self):
        dp, y, zl, core, x = self.g.pos

        @pl.when(zl < 3)
        def _():
            total = self.v[pl.ds(pl.multiple_of(16 * zl, 16), 16)].astype(F32)
            for k in range(1, 4):
                source = rem4(zl + k)
                self.one(1, self.ra.at[source], self.ra.at[source], self.twin_id(), 1 + source).wait_recv()
                total += self.ra[source].astype(F32)
            self.va[...] = total.astype(BF16)

            @pl.when(dp != y)
            def _():
                self.one(4, self.va, self.rb.at[dp], at(y, y, zl, core, x), 5 + dp).start()

    def others(self):
        dp, y, zl, core, x = self.g.pos
        for k in range(1, 16):
            chip = lax.rem(y * 4 + zl + k, 16)
            yield k, (dp, chip * 2 + core, x)

    def step5(self):
        dp, y, zl, core, x = self.g.pos

        @pl.when((zl < 3) & (dp == y))
        def _():
            total = self.va[...].astype(F32)
            for k in range(1, 4):
                source = rem4(dp + k)
                self.one(1, self.va, self.rb.at[source], self.twin_id(), 5 + source).wait_recv()
                total += self.rb[source].astype(F32)
            ref = self.f.at[core, pl.ds(pl.multiple_of(16 * zl, 16), 16)]
            ref[...] = total.astype(BF16)
            for k, target in self.others():
                self.one(15 + k, ref, ref, target, 9 + zl).start()

    def step6(self):
        dp, y, zl, core, x = self.g.pos
        whole = self.f.at[core]
        for t in range(3):

            @pl.when((dp != y) | (zl != t))
            def _():
                ref = self.f.at[core, pl.ds(16 * t, 16)]
                self.one(1, ref, ref, self.twin_id(), 9 + t).wait_recv()

        self.one(11, whole, whole, self.twin_id(), 13).start()

    def step7(self, out):
        dp, y, zl, core, x = self.g.pos
        other = self.f.at[1 - core]
        self.one(11, other, other, self.twin_id(), 13).wait_recv()
        out[:, :640] = self.f[0][:36].astype(F32)
        out[:, 640:] = self.f[1][:36, :512].astype(F32)

    def drain(self, att2, up2):
        dp, y, zl, core, x = self.g.pos
        third, whole = self.va, self.f.at[core]
        self.one(0, up2, up2, self.twin_id()).wait_send()
        self.one(12, att2, att2, self.twin_id()).wait_send()
        self.e2.drain()
        self.e1.drain()
        for t in range(3):

            @pl.when(zl != t)
            def _():
                self.one(1 + t, third, third, self.twin_id()).wait_send()

        @pl.when((zl < 3) & (dp != y))
        def _():
            self.one(4, third, third, self.twin_id()).wait_send()

        @pl.when((zl < 3) & (dp == y))
        def _():
            for k in range(1, 16):
                self.one(15 + k, third, third, self.twin_id()).wait_send()

        self.one(11, whole, whole, self.twin_id()).wait_send()


def halo_copies(low, high, from_low, from_high, sems, slot):
    dp, y, zl, core, x = coords()
    send, recv = sems
    return [
        pltpu.make_async_remote_copy(
            src_ref=src,
            dst_ref=dst,
            send_sem=send.at[slot, i],
            recv_sem=recv.at[slot, i],
            device_id=at(dp, y, zl, core, rem4(x + step)),
            device_id_type=MESH,
        )
        for i, (src, dst, step) in enumerate(((low, from_high, -1), (high, from_low, 1)))
    ]


def kernel(
    latents,
    upstream,
    modulation,
    space_qkv,
    space_out,
    time_qkv,
    time_out,
    pattern,
    time_mask,
    result,
    start_grad,
    out_grad,
    s,
):
    dp, y, zl, core, x = coords()
    gather = Gather((s["g0"], s["g1"], s["g2"]), s["g_send"], s["g_recv"])
    sems = (s["m_send"], s["m_recv"])
    halo_sems = (s["h_send"], s["h_recv"])

    def move(out, name, slot):
        return Move(out, s[name + "_out"], s[name + "_in"], sems, slot)

    lat_move = move(True, "lat", 0)
    up_move = move(True, "up", 1)
    att_move = move(True, "att", 2)
    back_att = move(False, "batt", 3)
    back_grad = move(False, "bgrad", 4)
    back_mid = move(False, "bmid", 5)

    def split(name, value):
        s[name + "_out"][...] = value.reshape(32, 4, value.shape[-1])

    def joined(name):
        return s[name + "_in"][...].reshape(ROWS, -1)
    total = Total(
        gather,
        [s[n] for n in ("term", "r1", "u", "r2", "v", "ra", "va", "rb", "f")],
        (s["t_send"], s["t_recv"]),
        (s["o_send"], s["o_recv"]),
    )

    place_own(gather, space_qkv, space_out, time_qkv, time_out)
    greet()
    for g in range(3):
        gather.zsend(g)
    low, high = pl.ds(0, 64), pl.ds(64, 64)
    edge = s["edge"]
    halo = halo_copies(latents.at[low], latents.at[high], edge.at[low], edge.at[high], halo_sems, 0)
    for copy in halo:
        copy.start()

    start = latents[...].astype(F32)
    gain_space = 1.0 + modulation[0:1, :]
    gain_time = 1.0 + modulation[1:2, :]
    inverse = inverse_of(start)
    s["inv_s"][...] = inverse
    s["normed"][:ROWS] = (start * inverse * gain_space).astype(BF16)
    split("lat", latents[...])
    split("up", upstream[...])

    gather.zpass(0)
    gather.open(0)
    gather.zpass(1)
    gather.zpass(2)
    gather.s1mid(0)
    gather.open(1)
    gather.mid(0, 0)
    gather.s1end(0)
    gather.open(2)
    lat_move.start()
    gather.mid(0, 1, 3)
    gather.s1mid(1)
    gather.mid(0, 2)
    up_move.start()
    gather.s1end(1)
    gather.mid(1, 0)
    for copy in halo:
        copy.wait_recv()
    start = edge[...].astype(F32)
    s["normed"][ROWS:] = (start * inverse_of(start) * gain_space).astype(BF16)
    s["sbias"][...] = space_bias(pattern, x)
    s["tbias"][...] = time_bias(time_mask)
    gather.s1mid(2)
    gather.fin(0, 0, 1, 3)
    gather.mid(1, 1, 3)
    gather.s1end(2)
    gather.fin(0, 2)
    gather.mid(2, 0)
    join_qkv(s["g0"], s["w0"], core)
    gather.end(0)
    join_qkv(s["g0"], s["w0"], 1 - core)
    gather.mid(1, 2)
    kv = s["kv"]
    s["q"][...] = dot(s["normed"][:ROWS], s["w0"][:, :WIDE]).astype(BF16)
    rows = dot(s["normed"][...], s["w0"][:, 512:])
    kv[0] = rows[:, 64 : 64 + WIDE].astype(BF16)
    kv[1] = rows[:, WIDE : 2 * WIDE].astype(BF16)
    gather.mid(2, 1, 3)
    attend(s["q"], kv.at[0], kv.at[1], s["sbias"][...], s["probs_s"], s["acc"])
    att = s["acc"][...].astype(BF16)
    split("att", att)
    att_move.start()
    gather.mid(2, 2)
    gather.fin(1, 0, 1, 3, 2)
    join_out(s["g1"], s["so"], s["to"], core)
    gather.end(1)
    join_out(s["g1"], s["so"], s["to"], 1 - core)
    gather.fin(2, 0, 1, 3)
    s["mid_f"][...] = latents[...].astype(F32) + dot(att[:, :WIDTH], s["so"][:, :D])
    gather.fin(2, 2)
    up_move.finish()
    total.share(s["up_in"], s["up2"])
    s["up"][...] = joined("up")
    s["tgrad"][:, :WIDTH] = dot_nt(s["up"][...], s["to"][:, :D]).astype(BF16)
    s["tgrad"][:, WIDTH:] = jnp.zeros((ROWS, WIDE - WIDTH), BF16)
    lat_move.finish()
    att_move.finish()

    middle = joined("lat").astype(F32) + dot(joined("att")[:, :WIDTH], s["so"][:, :D])
    inverse = inverse_of(middle)
    s["inv_t"][...] = inverse
    s["mid_p"][...] = middle
    join_qkv(s["g2"], s["w2"], core)
    gather.end(2)
    join_qkv(s["g2"], s["w2"], 1 - core)
    rows = dot((middle * inverse * gain_time).astype(BF16), s["w2"][...])
    s["tq"][...] = rows[:, :WIDE].astype(BF16)
    s["tk"][...] = rows[:, WIDTH : WIDTH + WIDE].astype(BF16)
    s["tv"][...] = rows[:, 2 * WIDTH : 2 * WIDTH + WIDE].astype(BF16)
    attend(s["tq"], s["tk"], s["tv"], s["tbias"][...], s["probs_t"], s["acc"])
    s["tatt"][...] = s["acc"][...].astype(BF16)
    total.give(s["tatt"], s["tatt2"])
    total.step1(s["tatt"], s["tatt2"], s["up"], s["up_in"], s["up2"])
    attend_back(s["tq"], s["tk"], s["tv"], s["probs_t"], s["tgrad"], s["acc"], s["tdk"], s["tdv"])
    s["grads"][:, :WIDTH] = s["acc"][:, :WIDTH].astype(BF16)
    s["grads"][:, WIDTH : 2 * WIDTH] = s["tdk"][:, :WIDTH].astype(BF16)
    s["grads"][:, 2 * WIDTH :] = s["tdv"][...].astype(BF16)
    grad = dot_nt(s["grads"][...], s["w2"][...])
    mid_grad = s["up"][...].astype(F32) + norm_back(s["mid_p"][...], s["inv_t"][...], gain_time, grad)
    s["mid_grad"][...] = mid_grad.astype(BF16)
    s["sgrad"][:, :WIDTH] = dot_nt(s["mid_grad"][...], s["so"][:, :D]).astype(BF16)
    s["sgrad"][:, WIDTH:] = jnp.zeros((ROWS, WIDE - WIDTH), BF16)
    split("bgrad", s["sgrad"][...])
    back_grad.start()
    split("batt", s["tatt"][...])
    split("bmid", s["mid_grad"][...])
    total.step2()
    back_att.start()
    gather.drain(0)
    gather.drain(1)
    total.step3()
    back_mid.start()
    gather.drain(2)
    for each in (lat_move, up_move, att_move):
        each.drain()
    back_grad.finish()
    s["sgrad"][...] = joined("bgrad")

    space_back_rim(s["q"], kv.at[1], s["probs_s"], s["sgrad"], s["ds"], s["rim32"])
    s["rim"][...] = s["rim32"][...].astype(BF16)
    out_rim, in_rim = s["rim"], s["rim_in"]
    rim = halo_copies(
        out_rim.at[:, low], out_rim.at[:, high], in_rim.at[:, low], in_rim.at[:, high], halo_sems, 1
    )
    for copy in rim:
        copy.start()
    total.step4()
    space_back_own(s["q"], kv.at[0], s["probs_s"], s["sgrad"], s["ds"], s["acc"], s["dkv"])
    grad = dot_nt(s["acc"][...].astype(BF16), s["w0"][:, :WIDE])
    total.step5()
    back_att.finish()
    result[...] = (s["mid_f"][...] + dot(joined("batt")[:, :WIDTH], s["to"][:, :D])).astype(BF16)
    for copy in rim:
        copy.wait_recv()
    own = (s["dkv"][...] + in_rim[...].astype(F32)).astype(BF16)
    s["grads"][:, WIDTH : 2 * WIDTH] = own[0][:, :WIDTH]
    s["grads"][:, 2 * WIDTH :] = own[1]
    s["grads"][:, 512:WIDTH] = jnp.zeros((ROWS, 64), BF16)
    grad += dot_nt(s["grads"][:, 512:], s["w0"][:, 512:])
    back_mid.finish()
    total.step6()
    start = latents[...].astype(F32)
    back = norm_back(start, s["inv_s"][...], gain_space, grad)
    start_grad[...] = (joined("bmid").astype(F32) + back).astype(BF16)
    for each in (back_att, back_grad, back_mid):
        each.drain()
    for copy in halo + rim:
        copy.wait_send()
    total.step7(out_grad)
    total.drain(s["tatt2"], s["up2"])


def scratch():
    def vmem(shape, dtype=BF16):
        return pltpu.VMEM(shape, dtype)

    dma = pltpu.SemaphoreType.DMA
    out = {f"g{g}": vmem((2, 4, 4, 9, 8, lanes)) for g, lanes in enumerate(LANES)}
    out.update(g_send=dma((3, 56)), g_recv=dma((3, 56)), m_send=dma((6, 32)), m_recv=dma((6, 32)))
    out.update(h_send=dma((2, 2)), h_recv=dma((2, 2)), t_send=dma((2, 3)), t_recv=dma((2, 3)))
    out.update(o_send=dma((32,)), o_recv=dma((16,)))
    out.update(w0=vmem((D, 1792)), w2=vmem((D, 1792)), so=vmem((WIDTH, 1280)), to=vmem((WIDTH, 1280)))
    for name, lanes in (("lat", D), ("up", D), ("att", WIDE), ("batt", WIDE), ("bgrad", WIDE), ("bmid", D)):
        out[name + "_out"], out[name + "_in"] = vmem((32, 4, lanes)), vmem((32, 4, lanes))
    for name in ("tatt", "tatt2", "q", "tq", "tk", "tv", "tgrad", "sgrad"):
        out[name] = vmem((ROWS, WIDE))
    out.update(normed=vmem((256, D)), mid_grad=vmem((ROWS, D)), up=vmem((ROWS, D)), up2=vmem((32, 4, D)))
    out.update(kv=vmem((2, 256, WIDE)), grads=vmem((ROWS, 1792)))
    out.update(rim=vmem((2, ROWS, WIDE)), rim_in=vmem((2, ROWS, WIDE)), edge=vmem((ROWS, D)))
    out.update(inv_s=vmem((ROWS, 1), F32), inv_t=vmem((ROWS, 1), F32), tbias=vmem((ROWS, ROWS), F32), sbias=vmem((ROWS, 256), F32))
    out.update(acc=vmem((ROWS, WIDE), F32), tdk=vmem((ROWS, WIDE), F32), tdv=vmem((ROWS, WIDE), F32))
    out.update(dkv=vmem((2, ROWS, WIDE), F32), rim32=vmem((2, ROWS, WIDE), F32), ds=vmem((HEADS, ROWS, 256)), mid_f=vmem((ROWS, D), F32), mid_p=vmem((ROWS, D), F32))
    out.update(probs_s=vmem((HEADS, ROWS, 256), F32), probs_t=vmem((HEADS, ROWS, ROWS), F32))
    block = (48, WIDE)
    out.update(term=vmem((4, 144, WIDE)), r1=vmem((4, 144, WIDE)))
    out.update(u=vmem((4,) + block), r2=vmem((4,) + block), v=vmem(block), ra=vmem((4, 16, WIDE)))
    out.update(va=vmem((16, WIDE)), rb=vmem((4, 16, WIDE)), f=vmem((2,) + block))
    return out


def local(
    latents,
    upstream,
    modulation,
    space_qkv,
    space_out,
    time_qkv,
    time_out,
    space_pattern,
    time_mask,
):
    shapes = scratch()
    names = list(shapes)

    def body(*refs):
        kernel(*refs[:12], dict(zip(names, refs[12:])))

    vmem = pl.BlockSpec(memory_space=pltpu.VMEM)
    smem = pl.BlockSpec(memory_space=pltpu.SMEM)
    result, start_grad, out_grad = pl.pallas_call(
        body,
        out_shape=[
            jax.ShapeDtypeStruct((ROWS, D), BF16),
            jax.ShapeDtypeStruct((ROWS, D), BF16),
            jax.ShapeDtypeStruct((36, D), F32),
        ],
        in_specs=[vmem] * 7 + [smem, vmem],
        out_specs=[vmem] * 3,
        scratch_shapes=list(shapes.values()),
        compiler_params=pltpu.CompilerParams(
            collective_id=0, has_side_effects=True, vmem_limit_bytes=60 << 20
        ),
    )(
        latents.reshape(ROWS, D),
        upstream.reshape(ROWS, D),
        modulation.reshape(2, D),
        space_qkv,
        space_out,
        time_qkv,
        time_out,
        space_pattern,
        time_mask,
    )
    return (result.reshape(latents.shape), start_grad.reshape(latents.shape), out_grad)


def solution(mesh):
    in_specs = (
        P("dp", "seq", "tile", None),
        P("dp", "seq", "tile", None),
        P("dp", None, None),
        P(("dp", "tile"), None),
        P(("dp", "tile"), None),
        P(("dp", "tile"), None),
        P(("dp", "tile"), None),
        P("tile", None),
        P(),
    )
    out_specs = (
        P("dp", "seq", "tile", None),
        P("dp", "seq", "tile", None),
        P(("dp", "tile"), None),
    )
    return jax.shard_map(local, mesh=mesh, in_specs=in_specs, out_specs=out_specs, check_vma=False)
```

```python
import jax
import jax.numpy as jnp
from jax import lax
from jax.experimental import pallas as pl
from jax.experimental.pallas import tpu as pltpu
from jax.sharding import PartitionSpec as P

HEADS = 8
HEAD_DIM = 72
WIDTH = HEADS * HEAD_DIM
WIDE = 640
D = 1152
ROWS = 128
EPSILON = 1e-06
MASKED = -1e30
SCALE = HEAD_DIM ** (-0.5)
BF16 = jnp.bfloat16
F32 = jnp.float32

MESH = pl.DeviceIdType.MESH
LANES = (896, 640, 896)


def coords():
    dp, seq, tile = lax.axis_index("dp"), lax.axis_index("seq"), lax.axis_index("tile")
    return dp, seq // 8, (seq // 2) % 4, seq % 2, tile


def at(dp, y, zl, core, tile):
    return (dp, (y * 4 + zl) * 2 + core, tile)


def rem4(value):
    return lax.rem(value + 8, 4)


class Gather:
    def __init__(self, bufs, send, recv):
        self.bufs, self.send, self.recv = bufs, send, recv
        dp, y, zl, core, x = self.pos = coords()
        self.first = core == 0
        self.p1 = jnp.where(self.first, y, x)
        self.p2 = jnp.where(self.first, x, y)
        self.q1 = jnp.where(self.first, x, y)
        self.q2 = jnp.where(self.first, y, x)

    def along1(self, place):
        dp, y, zl, core, x = self.pos
        place = rem4(place)
        return at(dp, jnp.where(self.first, place, y), zl, core, jnp.where(self.first, x, place))

    def along2(self, place):
        dp, y, zl, core, x = self.pos
        place = rem4(place)
        return at(dp, jnp.where(self.first, y, place), zl, core, jnp.where(self.first, place, x))

    def copy(self, g, ref, slot, target=None, recv_slot=None):
        return pltpu.make_async_remote_copy(
            src_ref=ref,
            dst_ref=ref,
            send_sem=self.send.at[g, slot],
            recv_sem=self.recv.at[g, slot if recv_slot is None else recv_slot],
            device_id=at(*self.pos) if target is None else target,
            device_id_type=MESH,
        )

    def block(self, g, i2, i1):
        return self.bufs[g].at[self.pos[3], rem4(i2), rem4(i1)]

    def own(self, g):
        return self.block(g, self.p2, self.p1)

    def third(self, g, t):
        return self.own(g).at[pl.ds(3 * t, 3)]

    def source(self, t):
        return rem4(self.pos[1] - t)

    def zsend(self, g):
        dp, y, zl, core, x = self.pos

        @pl.when((zl < 3) & (dp == self.source(zl)))
        def _():
            for k in range(1, 4):
                self.copy(g, self.third(g, zl), k - 1, at(rem4(dp + k), y, zl, core, x), 0).start()

    def neighbours(self):
        dp, y, zl, core, x = self.pos
        z = dp * 4 + zl
        for i, step in enumerate((1, -1, jnp.where(zl == 2, -2, 2))):
            other = lax.rem(z + step + 16, 16)
            yield i, other // 4, at(other // 4, y, lax.rem(other, 4), core, x)

    def zpass(self, g):
        dp, y, zl, core, x = self.pos

        @pl.when((zl < 3) & (dp != self.source(zl)))
        def _():
            self.copy(g, self.third(g, zl), 0, None, 0).wait_recv()

        for i, their, target in self.neighbours():

            @pl.when((zl < 3) & (their != self.source(zl)))
            def _():
                self.copy(g, self.third(g, zl), 16 + i, target, 1 + zl).start()

    def zdone(self, g):
        dp, y, zl, core, x = self.pos
        for t in range(3):

            @pl.when((dp != self.source(t)) & (zl != t))
            def _():
                self.copy(g, self.third(g, t), 0, None, 1 + t).wait_recv()

    def zend(self, g):
        dp, y, zl, core, x = self.pos

        @pl.when((zl < 3) & (dp == self.source(zl)))
        def _():
            for k in range(3):
                self.copy(g, self.third(g, zl), k).wait_send()

        for i, their, target in self.neighbours():

            @pl.when((zl < 3) & (their != self.source(zl)))
            def _():
                self.copy(g, self.third(g, zl), 16 + i).wait_send()

    def ring(self, g, axis, j, k):
        base = 4 if axis == 1 else 20 + 4 * j
        along, p = (self.along1, self.p1) if axis == 1 else (self.along2, self.p2)
        return base, along, p

    def push(self, g, axis, j=0):
        base, along, p = self.ring(g, axis, j, 0)
        ref = self.block(g, self.p2, self.p1 - j)
        self.copy(g, ref, base, along(p + 1)).start()
        self.copy(g, ref, base + 1, along(p - 1)).start()

    def seen(self, g, axis, j, k):
        return self.block(g, self.p2, self.p1 - k) if axis == 1 else self.block(g, self.p2 - k, self.p1 - j)

    def onward(self, g, axis, j, k):
        base, along, p = self.ring(g, axis, j, k)
        ref = self.seen(g, axis, j, k)
        if k == 1:
            self.copy(g, ref, base).wait_recv()
            self.copy(g, ref.at[pl.ds(0, 5)], base + 2, along(p + 1)).start()
        else:
            self.copy(g, ref, base + 1).wait_recv()
            self.copy(g, ref.at[pl.ds(5, 4)], base + 3, along(p - 1)).start()

    def last(self, g, axis, j):
        base, along, p = self.ring(g, axis, j, 2)
        ref = self.seen(g, axis, j, 2)
        self.copy(g, ref.at[pl.ds(0, 5)], base + 2).wait_recv()
        self.copy(g, ref.at[pl.ds(5, 4)], base + 3).wait_recv()

    def sent(self, g, axis, j):
        base, along, p = self.ring(g, axis, j, 0)
        self.copy(g, self.own(g), base).wait_send()
        self.copy(g, self.own(g), base + 1).wait_send()
        self.copy(g, self.own(g).at[pl.ds(0, 5)], base + 2).wait_send()
        self.copy(g, self.own(g).at[pl.ds(5, 4)], base + 3).wait_send()

    def twin(self, g, k, j):
        dp, y, zl, core, x = self.pos
        ref = self.block(g, self.p2 - k, self.p1 - j)
        self.copy(g, ref, 40 + 4 * j + k, at(dp, y, zl, 1 - core, x)).start()

    def round(self, g, j):
        self.push(g, 2, j)
        self.twin(g, 0, j)

    def open(self, g):
        self.zdone(g)
        self.push(g, 1)
        self.round(g, 0)

    def s1mid(self, g):
        for k in (1, 3):
            self.onward(g, 1, 0, k)
            self.round(g, k)

    def s1end(self, g):
        self.last(g, 1, 0)
        self.round(g, 2)

    def mid(self, g, *rounds):
        for j in rounds:
            for k in (1, 3):
                self.onward(g, 2, j, k)
                self.twin(g, k, j)

    def fin(self, g, *rounds):
        for j in rounds:
            self.last(g, 2, j)
            self.twin(g, 2, j)

    def end(self, g):
        for j in (0, 1, 3, 2):
            for k in (0, 1, 3, 2):
                ref = self.bufs[g].at[1 - self.pos[3], rem4(self.q2 - k), rem4(self.q1 - j)]
                self.copy(g, ref, 40 + 4 * j + k).wait_recv()

    def drain(self, g):
        self.zend(g)
        self.sent(g, 1, 0)
        for j in range(4):
            self.sent(g, 2, j)
            for k in range(4):
                self.copy(g, self.own(g), 40 + 4 * j + k).wait_send()


def greet():
    dp, y, zl, core, x = coords()
    seq = lax.axis_index("seq")
    barrier = pltpu.get_barrier_semaphore()

    def hello(target):
        pl.semaphore_signal(barrier, inc=1, device_id=target, device_id_type=MESH)

    def frame(k, carry):
        hello((dp, lax.rem(seq + k, 32), x))
        return carry

    lax.fori_loop(1, 32, frame, 0)
    for k in range(1, 4):
        hello(at(rem4(dp + k), y, zl, core, x))
        hello(at(dp, y, zl, core, rem4(x + k)))
    for step in (1, 3):
        hello(at(rem4(dp + step), y, 3 - zl, core, x))


def place_own(gather, space_qkv, space_out, time_qkv, time_out):
    dp, y, zl, core, x = gather.pos

    def put(g, block):
        block = block.reshape(9, 8, LANES[g])
        for t in range(3):

            @pl.when(dp == gather.source(t))
            def _():
                gather.third(g, t)[...] = block[3 * t : 3 * t + 3]

    for half in range(2):

        @pl.when(core == half)
        def _():
            for g, ref in ((0, space_qkv), (2, time_qkv)):
                if half == 0:
                    block = ref[:, :896]
                else:
                    block = jnp.concatenate([ref[:, 896:], jnp.zeros((72, 64), BF16)], axis=1)
                put(g, block)
            block = jnp.concatenate([space_out[...].astype(F32), time_out[...].astype(F32)], axis=0)
            if half == 0:
                block = block[:, :640]
            else:
                block = jnp.concatenate([block[:, 640:], jnp.zeros((72, 128), F32)], axis=1)
            put(1, block.astype(BF16))


class Exchange:
    def __init__(self, n, me, target, block, slot, send, recv):
        self.n, self.me, self.target = n, me, target
        self.block, self.slot, self.sems = block, slot, (send, recv)

    def copy(self, k, src, dst, target):
        return pltpu.make_async_remote_copy(
            src_ref=src,
            dst_ref=dst,
            send_sem=self.sems[0].at[k - 1],
            recv_sem=self.sems[1].at[k - 1],
            device_id=target,
            device_id_type=MESH,
        )

    def start(self):
        for k in (2, 1, 3):
            other = lax.rem(self.me + k, self.n)
            self.copy(k, self.block(other), self.slot(self.me), self.target(other)).start()

    def wait(self):
        for k in range(1, self.n):
            source = lax.rem(self.me + self.n - k, self.n)
            self.copy(k, self.slot(source), self.slot(source), self.target(source)).wait_recv()

    def drain(self):
        for k in range(1, self.n):
            other = lax.rem(self.me + k, self.n)
            self.copy(k, self.block(other), self.slot(self.me), self.target(other)).wait_send()


def dot(a, b):
    return jnp.dot(a, b, preferred_element_type=F32)


def dot_nt(a, b):
    return lax.dot_general(a, b, (((1,), (1,)), ((), ())), preferred_element_type=F32)


def dot_tn(a, b):
    return lax.dot_general(a, b, (((0,), (0,)), ((), ())), preferred_element_type=F32)


def iota(shape, axis):
    return lax.broadcasted_iota(jnp.int32, shape, axis)


class Move:
    def __init__(self, out, source, target, sems, slot):
        self.out, self.source, self.target, self.sems, self.slot = out, source, target, sems, slot
        self.tile, self.dp, self.seq = lax.axis_index("tile"), lax.axis_index("dp"), lax.axis_index("seq")

    def patches(self, seq):
        return (seq & 7) * 4 + (seq >> 3)

    def src(self, other):
        return self.source.at[self.patches(other) if self.out else other]

    def dst(self, owner):
        return self.target.at[owner if self.out else self.patches(owner)]

    def copy(self, k, other, owner):
        send, recv = self.sems
        return pltpu.make_async_remote_copy(
            src_ref=self.src(other),
            dst_ref=self.dst(owner),
            send_sem=send.at[self.slot, k],
            recv_sem=recv.at[self.slot, k],
            device_id=(self.dp, other, self.tile),
            device_id_type=MESH,
        )

    def each(self, step):
        def body(k, carry):
            step(k)
            return carry

        lax.fori_loop(1, 32, body, 0)

    def start(self):
        self.each(lambda k: self.copy(k, lax.rem(self.seq + k, 32), self.seq).start())
        self.dst(self.seq)[...] = self.src(self.seq)[...]

    def finish(self):
        self.each(lambda k: self.copy(k, self.seq, lax.rem(self.seq + 32 - k, 32)).wait_recv())

    def drain(self):
        self.each(lambda k: self.copy(k, self.seq, self.seq).wait_send())


def inverse_of(values):
    return lax.rsqrt(jnp.sum(values * values, axis=-1, keepdims=True) * (1.0 / D) + EPSILON)


def norm_back(values, inverse, gain, grad):
    scaled = grad * gain
    cubed = inverse * inverse * inverse
    mean = jnp.sum(scaled * values, axis=-1, keepdims=True) * (1.0 / D)
    return inverse * scaled - values * (cubed * mean)


def span(h):
    low, high = h * HEAD_DIM, (h + 1) * HEAD_DIM
    begin, end = low // 128 * 128, -(-high // 128) * 128
    lane = iota((1, end - begin), 1) + begin
    keep = ((lane >= low) & (lane < high)).astype(F32).astype(BF16)
    return slice(begin, end), keep


def attend(q, k, v, bias, probs, out):
    out[...] = jnp.zeros_like(out)
    for h in range(HEADS):
        lanes, keep = span(h)
        scores = dot_nt(q[:, lanes] * keep, k[:, lanes]) * SCALE + bias
        raised = jnp.exp(scores - jnp.max(scores, axis=-1, keepdims=True))
        p = raised * (1.0 / jnp.sum(raised, axis=-1, keepdims=True))
        probs[h] = p
        out[:, lanes] += dot(p.astype(BF16), v[:, lanes] * keep)


def attend_back(q, k, v, probs, grad, dq, dk, dv):
    for ref in (dq, dk, dv):
        ref[...] = jnp.zeros_like(ref)
    for h in range(HEADS):
        lanes, keep = span(h)
        o = grad[:, lanes] * keep
        p = probs[h]
        dp = dot_nt(o, v[:, lanes])
        delta = jnp.sum(p * dp, axis=-1, keepdims=True)
        ds = (p * (dp - delta) * SCALE).astype(BF16)
        dq[:, lanes] += dot(ds, k[:, lanes] * keep)
        dk[:, lanes] += dot_tn(ds, q[:, lanes] * keep)
        dv[:, lanes] += dot_tn(p.astype(BF16), o)


def space_back_rim(q, v, probs, grad, ds_all, rim):
    rim[...] = jnp.zeros_like(rim)
    for h in range(HEADS):
        lanes, keep = span(h)
        o = grad[:, lanes] * keep
        p = probs[h]
        dp = dot_nt(o, v[:, lanes])
        delta = jnp.sum(p * dp, axis=-1, keepdims=True)
        ds = (p * (dp - delta) * SCALE).astype(BF16)
        ds_all[h] = ds
        rim[0, :, lanes] += dot_tn(ds[:, 128:], q[:, lanes] * keep)
        rim[1, :, lanes] += dot_tn(p[:, 128:].astype(BF16), o)


def space_back_own(q, k, probs, grad, ds_all, dq, dkv):
    dq[...] = jnp.zeros_like(dq)
    dkv[...] = jnp.zeros_like(dkv)
    for h in range(HEADS):
        lanes, keep = span(h)
        ds = ds_all[h]
        dq[:, lanes] += dot(ds, k[:, lanes] * keep)
        dkv[0, :, lanes] += dot_tn(ds[:, :128], q[:, lanes] * keep)
        dkv[1, :, lanes] += dot_tn(probs[h, :, :128].astype(BF16), grad[:, lanes] * keep)


def time_bias(time_mask):
    row, frame = iota((ROWS, 32), 0), iota((ROWS, 32), 1)
    spread = ((row >> 2) == frame).astype(F32).astype(BF16)
    mask = (time_mask[...] == 1).astype(F32).astype(BF16)
    mask = dot_nt(dot(spread, mask).astype(BF16), spread)
    a, b = iota((ROWS, ROWS), 0), iota((ROWS, ROWS), 1)
    fa, fb = a >> 2, b >> 2
    ok = ((a & 3) == (b & 3)) & ((fa == fb) | ((fb < fa) & (mask > 0.5)))
    return jnp.where(ok, 0.0, MASKED)


def space_bias(pattern, x):
    part = iota((1, 256), 1) >> 6
    slot = jnp.where(part < 2, part + 1, jnp.where(part == 2, 0, 3))
    sides = []
    for row in range(2):
        bias = jnp.zeros((1, 256), F32)
        for r in range(4):
            block = 2 * x - 1 + r
            inside = (block >= 0) & (block < 8)
            seen = (pattern[row, r] == 1) | (r == row + 1)
            value = jnp.where(inside & seen, 0.0, MASKED)
            bias = jnp.where(slot == r, value, bias)
        sides.append(bias)
    return jnp.where(iota((ROWS, 256), 0) < 64, sides[0], sides[1])


def shard(buf, half, zh, x):
    first = half == 0
    parts = []
    for t in range(3):
        share = rem4(zh + t)
        part = buf[half, jnp.where(first, x, share), jnp.where(first, share, x)]
        parts.append(part[3 * t : 3 * t + 3])
    return jnp.concatenate(parts, axis=0).reshape(72, buf.shape[-1])


def join_qkv(buf, whole, half):
    lanes = pl.ds(pl.multiple_of(half * 896, 128), 896)

    def body(i, carry):
        zh, x = i >> 1, (i & 1) * 2
        rows = pl.ds(pl.multiple_of(i * 144, 16), 144)
        pair = jnp.concatenate([shard(buf, half, zh, x), shard(buf, half, zh, x + 1)], axis=0)
        whole[rows, lanes] = pair
        return carry

    lax.fori_loop(0, 8, body, 0)


def join_out(buf, space, time, half):
    lanes = pl.ds(pl.multiple_of(half * 640, 128), 640)

    def body(zh, carry):
        rows = pl.ds(pl.multiple_of(zh * 144, 16), 144)
        blocks = [shard(buf, half, zh, x).astype(F32) for x in range(4)]
        for ref, low in ((space, 0), (time, 36)):
            part = jnp.concatenate([block[low : low + 36] for block in blocks], axis=0)
            ref[rows, lanes] = part.astype(BF16)
        return carry

    lax.fori_loop(0, 4, body, 0)


class Total:
    def __init__(self, gather, refs, sems, small):
        self.g = gather
        self.term, self.r1, self.u, self.r2, self.v, self.ra, self.va, self.rb, self.f = refs
        send, recv = sems
        self.small = small
        dp, y, zl, core, x = gather.pos
        term, u, r1, r2 = self.term, self.u, self.r1, self.r2
        self.e2 = Exchange(
            4, gather.p2, gather.along2, lambda i: term.at[i], lambda i: r1.at[i], send.at[0], recv.at[0]
        )
        self.e1 = Exchange(
            4, gather.p1, gather.along1, lambda i: u.at[i], lambda i: r2.at[i], send.at[1], recv.at[1]
        )

    def one(self, slot, src, dst, target, recv_slot=None):
        send, recv = self.small
        return pltpu.make_async_remote_copy(
            src_ref=src,
            dst_ref=dst,
            send_sem=send.at[slot],
            recv_sem=recv.at[slot if recv_slot is None else recv_slot],
            device_id=target,
            device_id_type=MESH,
        )

    def twin_id(self):
        dp, y, zl, core, x = self.g.pos
        return at(dp, y, zl, 1 - core, x)

    def share(self, up, up2):
        self.one(0, up, up2, self.twin_id()).start()

    def give(self, att, att2):
        self.one(12, att, att2, self.twin_id(), 14).start()

    def step1(self, att, att2, up, up_in, up2):
        dp, y, zl, core, x = self.g.pos
        for half in range(2):

            @pl.when(core == half)
            def _():
                lanes = slice(0, 640) if half == 0 else slice(640, D)
                term = dot_tn(att[:, :WIDTH], up[:, lanes])
                self.one(0, up_in, up2, self.twin_id()).wait_recv()
                self.one(12, att, att2, self.twin_id(), 14).wait_recv()
                term += dot_tn(att2[:, :WIDTH], up2[:, :, lanes].reshape(ROWS, -1))
                if half == 1:
                    term = jnp.concatenate([term, jnp.zeros((WIDTH, 128), F32)], axis=1)
                for i in range(4):
                    if half == 0:
                        rows = [term[36 * (4 * j + i) : 36 * (4 * j + i) + 36] for j in range(4)]
                        self.term[i] = jnp.concatenate(rows, axis=0).astype(BF16)
                    else:
                        self.term[i] = term[144 * i : 144 * i + 144].astype(BF16)

        self.e2.start()

    def step2(self):
        dp, y, zl, core, x = self.g.pos
        self.e2.wait()
        p = self.g.p2
        total = self.term[p].astype(F32)
        for k in range(1, 4):
            total += self.r1[rem4(p + k)].astype(F32)
        for i in range(4):
            block = jnp.concatenate([total[36 * i : 36 * i + 36], jnp.zeros((12, 640), F32)], axis=0)
            self.u[i] = block.astype(BF16)
        self.e1.start()

    def step3(self):
        dp, y, zl, core, x = self.g.pos
        self.e1.wait()
        p = self.g.p1
        total = self.u[p].astype(F32)
        for k in range(1, 4):
            total += self.r2[rem4(p + k)].astype(F32)
        self.v[...] = total.astype(BF16)
        for t in range(3):

            @pl.when(zl != t)
            def _():
                ref = self.v.at[pl.ds(16 * t, 16)]
                self.one(1 + t, ref, self.ra.at[zl], at(dp, y, t, core, x), 1 + zl).start()

    def step4(self):
        dp, y, zl, core, x = self.g.pos

        @pl.when(zl < 3)
        def _():
            total = self.v[pl.ds(pl.multiple_of(16 * zl, 16), 16)].astype(F32)
            for k in range(1, 4):
                source = rem4(zl + k)
                self.one(1, self.ra.at[source], self.ra.at[source], self.twin_id(), 1 + source).wait_recv()
                total += self.ra[source].astype(F32)
            self.va[...] = total.astype(BF16)

            @pl.when(dp != y)
            def _():
                self.one(4, self.va, self.rb.at[dp], at(y, y, zl, core, x), 5 + dp).start()

    def others(self):
        dp, y, zl, core, x = self.g.pos
        for k in range(1, 16):
            chip = lax.rem(y * 4 + zl + k, 16)
            yield k, (dp, chip * 2 + core, x)

    def step5(self):
        dp, y, zl, core, x = self.g.pos

        @pl.when((zl < 3) & (dp == y))
        def _():
            total = self.va[...].astype(F32)
            for k in range(1, 4):
                source = rem4(dp + k)
                self.one(1, self.va, self.rb.at[source], self.twin_id(), 5 + source).wait_recv()
                total += self.rb[source].astype(F32)
            ref = self.f.at[core, pl.ds(pl.multiple_of(16 * zl, 16), 16)]
            ref[...] = total.astype(BF16)
            for k, target in self.others():
                self.one(15 + k, ref, ref, target, 9 + zl).start()

    def step6(self):
        dp, y, zl, core, x = self.g.pos
        whole = self.f.at[core]
        for t in range(3):

            @pl.when((dp != y) | (zl != t))
            def _():
                ref = self.f.at[core, pl.ds(16 * t, 16)]
                self.one(1, ref, ref, self.twin_id(), 9 + t).wait_recv()

        self.one(11, whole, whole, self.twin_id(), 13).start()

    def step7(self, out):
        dp, y, zl, core, x = self.g.pos
        other = self.f.at[1 - core]
        self.one(11, other, other, self.twin_id(), 13).wait_recv()
        out[:, :640] = self.f[0][:36].astype(F32)
        out[:, 640:] = self.f[1][:36, :512].astype(F32)

    def drain(self, att2, up2):
        dp, y, zl, core, x = self.g.pos
        third, whole = self.va, self.f.at[core]
        self.one(0, up2, up2, self.twin_id()).wait_send()
        self.one(12, att2, att2, self.twin_id()).wait_send()
        self.e2.drain()
        self.e1.drain()
        for t in range(3):

            @pl.when(zl != t)
            def _():
                self.one(1 + t, third, third, self.twin_id()).wait_send()

        @pl.when((zl < 3) & (dp != y))
        def _():
            self.one(4, third, third, self.twin_id()).wait_send()

        @pl.when((zl < 3) & (dp == y))
        def _():
            for k in range(1, 16):
                self.one(15 + k, third, third, self.twin_id()).wait_send()

        self.one(11, whole, whole, self.twin_id()).wait_send()


def halo_copies(low, high, from_low, from_high, sems, slot):
    dp, y, zl, core, x = coords()
    send, recv = sems
    return [
        pltpu.make_async_remote_copy(
            src_ref=src,
            dst_ref=dst,
            send_sem=send.at[slot, i],
            recv_sem=recv.at[slot, i],
            device_id=at(dp, y, zl, core, rem4(x + step)),
            device_id_type=MESH,
        )
        for i, (src, dst, step) in enumerate(((low, from_high, -1), (high, from_low, 1)))
    ]


def kernel(
    latents,
    upstream,
    modulation,
    space_qkv,
    space_out,
    time_qkv,
    time_out,
    pattern,
    time_mask,
    result,
    start_grad,
    out_grad,
    s,
):
    dp, y, zl, core, x = coords()
    gather = Gather((s["g0"], s["g1"], s["g2"]), s["g_send"], s["g_recv"])
    sems = (s["m_send"], s["m_recv"])
    halo_sems = (s["h_send"], s["h_recv"])

    def move(out, name, slot):
        return Move(out, s[name + "_out"], s[name + "_in"], sems, slot)

    lat_move = move(True, "lat", 0)
    up_move = move(True, "up", 1)
    att_move = move(True, "att", 2)
    back_att = move(False, "batt", 3)
    back_grad = move(False, "bgrad", 4)
    back_mid = move(False, "bmid", 5)

    def split(name, value):
        s[name + "_out"][...] = value.reshape(32, 4, value.shape[-1])

    def joined(name):
        return s[name + "_in"][...].reshape(ROWS, -1)
    total = Total(
        gather,
        [s[n] for n in ("term", "r1", "u", "r2", "v", "ra", "va", "rb", "f")],
        (s["t_send"], s["t_recv"]),
        (s["o_send"], s["o_recv"]),
    )

    greet()
    place_own(gather, space_qkv, space_out, time_qkv, time_out)
    pl.semaphore_wait(pltpu.get_barrier_semaphore(), 39)
    for g in range(3):
        gather.zsend(g)
    low, high = pl.ds(0, 64), pl.ds(64, 64)
    edge = s["edge"]
    halo = halo_copies(latents.at[low], latents.at[high], edge.at[low], edge.at[high], halo_sems, 0)
    for copy in halo:
        copy.start()

    start = latents[...].astype(F32)
    gain_space = 1.0 + modulation[0:1, :]
    gain_time = 1.0 + modulation[1:2, :]
    inverse = inverse_of(start)
    s["inv_s"][...] = inverse
    s["normed"][:ROWS] = (start * inverse * gain_space).astype(BF16)
    split("lat", latents[...])
    split("up", upstream[...])

    gather.zpass(0)
    gather.open(0)
    gather.zpass(1)
    gather.zpass(2)
    gather.s1mid(0)
    gather.open(1)
    up_move.start()
    lat_move.start()
    gather.mid(0, 0)
    gather.s1end(0)
    gather.open(2)
    gather.mid(0, 1, 3)
    gather.s1mid(1)
    gather.mid(0, 2)
    gather.s1end(1)
    gather.mid(1, 0)
    for copy in halo:
        copy.wait_recv()
    start = edge[...].astype(F32)
    s["normed"][ROWS:] = (start * inverse_of(start) * gain_space).astype(BF16)
    s["sbias"][...] = space_bias(pattern, x)
    s["tbias"][...] = time_bias(time_mask)
    gather.s1mid(2)
    gather.fin(0, 0, 1, 3)
    gather.mid(1, 1, 3)
    gather.s1end(2)
    gather.fin(0, 2)
    gather.mid(2, 0)
    join_qkv(s["g0"], s["w0"], core)
    gather.end(0)
    join_qkv(s["g0"], s["w0"], 1 - core)
    gather.mid(1, 2)
    kv = s["kv"]
    s["q"][...] = dot(s["normed"][:ROWS], s["w0"][:, :WIDE]).astype(BF16)
    rows = dot(s["normed"][...], s["w0"][:, 512:])
    kv[0] = rows[:, 64 : 64 + WIDE].astype(BF16)
    kv[1] = rows[:, WIDE : 2 * WIDE].astype(BF16)
    gather.mid(2, 1, 3)
    attend(s["q"], kv.at[0], kv.at[1], s["sbias"][...], s["probs_s"], s["acc"])
    att = s["acc"][...].astype(BF16)
    split("att", att)
    att_move.start()
    gather.mid(2, 2)
    gather.fin(1, 0, 1, 3, 2)
    join_out(s["g1"], s["so"], s["to"], core)
    gather.end(1)
    join_out(s["g1"], s["so"], s["to"], 1 - core)
    gather.fin(2, 0, 1, 3)
    s["mid_f"][...] = latents[...].astype(F32) + dot(att[:, :WIDTH], s["so"][:, :D])
    gather.fin(2, 2)
    join_qkv(s["g2"], s["w2"], core)
    up_move.finish()
    total.share(s["up_in"], s["up2"])
    s["up"][...] = joined("up")
    s["tgrad"][:, :WIDTH] = dot_nt(s["up"][...], s["to"][:, :D]).astype(BF16)
    s["tgrad"][:, WIDTH:] = jnp.zeros((ROWS, WIDE - WIDTH), BF16)
    lat_move.finish()
    att_move.finish()

    middle = joined("lat").astype(F32) + dot(joined("att")[:, :WIDTH], s["so"][:, :D])
    inverse = inverse_of(middle)
    s["inv_t"][...] = inverse
    s["mid_p"][...] = middle
    gather.end(2)
    join_qkv(s["g2"], s["w2"], 1 - core)
    rows = dot((middle * inverse * gain_time).astype(BF16), s["w2"][...])
    s["tq"][...] = rows[:, :WIDE].astype(BF16)
    s["tk"][...] = rows[:, WIDTH : WIDTH + WIDE].astype(BF16)
    s["tv"][...] = rows[:, 2 * WIDTH : 2 * WIDTH + WIDE].astype(BF16)
    attend(s["tq"], s["tk"], s["tv"], s["tbias"][...], s["probs_t"], s["acc"])
    s["tatt"][...] = s["acc"][...].astype(BF16)
    total.give(s["tatt"], s["tatt2"])
    total.step1(s["tatt"], s["tatt2"], s["up"], s["up_in"], s["up2"])
    attend_back(s["tq"], s["tk"], s["tv"], s["probs_t"], s["tgrad"], s["acc"], s["tdk"], s["tdv"])
    s["grads"][:, :WIDTH] = s["acc"][:, :WIDTH].astype(BF16)
    s["grads"][:, WIDTH : 2 * WIDTH] = s["tdk"][:, :WIDTH].astype(BF16)
    s["grads"][:, 2 * WIDTH :] = s["tdv"][...].astype(BF16)
    grad = dot_nt(s["grads"][...], s["w2"][...])
    mid_grad = s["up"][...].astype(F32) + norm_back(s["mid_p"][...], s["inv_t"][...], gain_time, grad)
    s["mid_grad"][...] = mid_grad.astype(BF16)
    s["sgrad"][:, :WIDTH] = dot_nt(s["mid_grad"][...], s["so"][:, :D]).astype(BF16)
    s["sgrad"][:, WIDTH:] = jnp.zeros((ROWS, WIDE - WIDTH), BF16)
    split("bgrad", s["sgrad"][...])
    back_grad.start()
    split("batt", s["tatt"][...])
    split("bmid", s["mid_grad"][...])
    total.step2()
    back_att.start()
    gather.drain(0)
    gather.drain(1)
    total.step3()
    back_mid.start()
    gather.drain(2)
    for each in (lat_move, up_move, att_move):
        each.drain()
    back_grad.finish()
    s["sgrad"][...] = joined("bgrad")

    space_back_rim(s["q"], kv.at[1], s["probs_s"], s["sgrad"], s["ds"], s["rim32"])
    s["rim"][...] = s["rim32"][...].astype(BF16)
    out_rim, in_rim = s["rim"], s["rim_in"]
    rim = halo_copies(
        out_rim.at[:, low], out_rim.at[:, high], in_rim.at[:, low], in_rim.at[:, high], halo_sems, 1
    )
    for copy in rim:
        copy.start()
    total.step4()
    space_back_own(s["q"], kv.at[0], s["probs_s"], s["sgrad"], s["ds"], s["acc"], s["dkv"])
    grad = dot_nt(s["acc"][...].astype(BF16), s["w0"][:, :WIDE])
    total.step5()
    back_att.finish()
    result[...] = (s["mid_f"][...] + dot(joined("batt")[:, :WIDTH], s["to"][:, :D])).astype(BF16)
    for copy in rim:
        copy.wait_recv()
    own = (s["dkv"][...] + in_rim[...].astype(F32)).astype(BF16)
    s["grads"][:, WIDTH : 2 * WIDTH] = own[0][:, :WIDTH]
    s["grads"][:, 2 * WIDTH :] = own[1]
    s["grads"][:, 512:WIDTH] = jnp.zeros((ROWS, 64), BF16)
    grad += dot_nt(s["grads"][:, 512:], s["w0"][:, 512:])
    back_mid.finish()
    total.step6()
    start = latents[...].astype(F32)
    back = norm_back(start, s["inv_s"][...], gain_space, grad)
    start_grad[...] = (joined("bmid").astype(F32) + back).astype(BF16)
    for each in (back_att, back_grad, back_mid):
        each.drain()
    for copy in halo + rim:
        copy.wait_send()
    total.step7(out_grad)
    total.drain(s["tatt2"], s["up2"])


def scratch():
    def vmem(shape, dtype=BF16):
        return pltpu.VMEM(shape, dtype)

    dma = pltpu.SemaphoreType.DMA
    out = {f"g{g}": vmem((2, 4, 4, 9, 8, lanes)) for g, lanes in enumerate(LANES)}
    out.update(g_send=dma((3, 56)), g_recv=dma((3, 56)), m_send=dma((6, 32)), m_recv=dma((6, 32)))
    out.update(h_send=dma((2, 2)), h_recv=dma((2, 2)), t_send=dma((2, 3)), t_recv=dma((2, 3)))
    out.update(o_send=dma((32,)), o_recv=dma((16,)))
    out.update(w0=vmem((D, 1792)), w2=vmem((D, 1792)), so=vmem((WIDTH, 1280)), to=vmem((WIDTH, 1280)))
    for name, lanes in (("lat", D), ("up", D), ("att", WIDE), ("batt", WIDE), ("bgrad", WIDE), ("bmid", D)):
        out[name + "_out"], out[name + "_in"] = vmem((32, 4, lanes)), vmem((32, 4, lanes))
    for name in ("tatt", "tatt2", "q", "tq", "tk", "tv", "tgrad", "sgrad"):
        out[name] = vmem((ROWS, WIDE))
    out.update(normed=vmem((256, D)), mid_grad=vmem((ROWS, D)), up=vmem((ROWS, D)), up2=vmem((32, 4, D)))
    out.update(kv=vmem((2, 256, WIDE)), grads=vmem((ROWS, 1792)))
    out.update(rim=vmem((2, ROWS, WIDE)), rim_in=vmem((2, ROWS, WIDE)), edge=vmem((ROWS, D)))
    out.update(inv_s=vmem((ROWS, 1), F32), inv_t=vmem((ROWS, 1), F32), tbias=vmem((ROWS, ROWS), F32), sbias=vmem((ROWS, 256), F32))
    out.update(acc=vmem((ROWS, WIDE), F32), tdk=vmem((ROWS, WIDE), F32), tdv=vmem((ROWS, WIDE), F32))
    out.update(dkv=vmem((2, ROWS, WIDE), F32), rim32=vmem((2, ROWS, WIDE), F32), ds=vmem((HEADS, ROWS, 256)), mid_f=vmem((ROWS, D), F32), mid_p=vmem((ROWS, D), F32))
    out.update(probs_s=vmem((HEADS, ROWS, 256), F32), probs_t=vmem((HEADS, ROWS, ROWS), F32))
    block = (48, WIDE)
    out.update(term=vmem((4, 144, WIDE)), r1=vmem((4, 144, WIDE)))
    out.update(u=vmem((4,) + block), r2=vmem((4,) + block), v=vmem(block), ra=vmem((4, 16, WIDE)))
    out.update(va=vmem((16, WIDE)), rb=vmem((4, 16, WIDE)), f=vmem((2,) + block))
    return out


def local(
    latents,
    upstream,
    modulation,
    space_qkv,
    space_out,
    time_qkv,
    time_out,
    space_pattern,
    time_mask,
):
    shapes = scratch()
    names = list(shapes)

    def body(*refs):
        kernel(*refs[:12], dict(zip(names, refs[12:])))

    vmem = pl.BlockSpec(memory_space=pltpu.VMEM)
    smem = pl.BlockSpec(memory_space=pltpu.SMEM)
    result, start_grad, out_grad = pl.pallas_call(
        body,
        out_shape=[
            jax.ShapeDtypeStruct((ROWS, D), BF16),
            jax.ShapeDtypeStruct((ROWS, D), BF16),
            jax.ShapeDtypeStruct((36, D), F32),
        ],
        in_specs=[vmem] * 7 + [smem, vmem],
        out_specs=[vmem] * 3,
        scratch_shapes=list(shapes.values()),
        compiler_params=pltpu.CompilerParams(
            collective_id=0, has_side_effects=True, vmem_limit_bytes=60 << 20
        ),
    )(
        latents.reshape(ROWS, D),
        upstream.reshape(ROWS, D),
        modulation.reshape(2, D),
        space_qkv,
        space_out,
        time_qkv,
        time_out,
        space_pattern,
        time_mask,
    )
    return (result.reshape(latents.shape), start_grad.reshape(latents.shape), out_grad)


def solution(mesh):
    in_specs = (
        P("dp", "seq", "tile", None),
        P("dp", "seq", "tile", None),
        P("dp", None, None),
        P(("dp", "tile"), None),
        P(("dp", "tile"), None),
        P(("dp", "tile"), None),
        P(("dp", "tile"), None),
        P("tile", None),
        P(),
    )
    out_specs = (
        P("dp", "seq", "tile", None),
        P("dp", "seq", "tile", None),
        P(("dp", "tile"), None),
    )
    return jax.shard_map(local, mesh=mesh, in_specs=in_specs, out_specs=out_specs, check_vma=False)
```
